256 devices in a mesh: gx: 8 (over z), gy: 4 (over x), gz: 8 (over y, core).
Axes of the slice: x: 4, y: 4, z: 8, core: 2. Of those that a mesh axis runs over, the one named last changes fastest.
Arguments:
- fields: float32 [5, 64, 32, 1024], P(None, 'gx', 'gy', 'gz'), may hold values from -4 to 4
- tracer_ref: float32 [3, 1048576], P(None, ('gx', 'gy', 'gz')), may hold values from -1 to 1
- host_element: int32 [1048576], P(('gx', 'gy', 'gz')), may hold values from 0 to 15
- block_owner: int32 [8192, 1], P(('gx', 'gy', 'gz')), may hold values from 0 to 31; in each aligned block of 32 rows (0 to 31, 32 to 63, ...) at most 2 rows name the same one
Outputs:
- fields_out: float32 [5, 64, 32, 1024], P(None, 'gx', 'gy', 'gz')
- moved_ref: float32 [3, 1048576], P(None, ('gx', 'gy', 'gz'))
The draws below stay inside these ranges and needn't reach their ends.
Inputs may be any that keep to these rules, and one draw needn't show every extreme that they name: `host_element`: element number of the tracer's host within the block of 1 x 1 x 16 elements of its owner, numbered (ex * 1 + ey) * 16 + ez. `block_owner`: owner of a block in its own gx slab, numbered gy * 8 + gz. Among the 32 blocks of one device at most 2 have the same owner, and some device has exactly 2 blocks with one owner.
All inputs are finite; a program needn't handle non-finite values.
Results may differ from the reference program's by a relative error of at most 0.0054.
Values sent between devices are 32-bit elements; how exact they have to be, the bound alone decides.
A program may use at most 64 MiB of HBM per device.

```python
import math
import jax
import jax.numpy as jnp
import numpy as np
from jax import lax

EX = 1
EY = 1
EZ = 16
NB = 32
CAP = 2
NX = 64
NY = 32
NZ = 1024
BLOCKS = 8192
TRACERS = 1048576
N_GY = 4
N_GZ = 8


def place_ends(values, own_key, least, high):
    longest = values.shape.index(max(values.shape))
    spots = []
    for shift in (0, 1):
        where = [jax.random.randint(jax.random.fold_in(own_key, axis), (), 0, length) for axis, length in enumerate(values.shape)]
        where[longest] = (where[longest] + shift) % values.shape[longest]
        spots.append(tuple(where))
    return values.at[spots[0]].set(least).at[spots[1]].set(high)


def block_scale(stream_key, dims, cuts, smallest, top_value):
    factor_of = 1.0
    for axis_at, shards_of in cuts:
        draws = jax.random.uniform(jax.random.fold_in(jax.random.fold_in(stream_key, 6), axis_at), (shards_of,), jnp.float32, smallest / len(cuts), top_value / len(cuts))
        factor_of = factor_of * jnp.repeat(jnp.exp(draws), dims[axis_at] // shards_of).reshape((-1,) + (1,) * (len(dims) - 1 - axis_at))
    return factor_of


def assign_block(stream_key, own, number, rows, count, top, most, lean):
    ranking = jax.random.permutation(stream_key, count)
    crowded, ordinary = shares(count, rows * top, most, lean, True), shares(count, rows * top, most, lean, False)
    places = jnp.arange(count)

    def named(sizes, turn):
        used = int((sizes > 0).sum())
        fixed = max(1, used // 4)
        moved = fixed + (places - fixed + turn * (used - fixed)) % max(1, count - fixed)
        return jnp.zeros((count,), jnp.int32).at[ranking[jnp.where(places < fixed, places, moved)]].set(jnp.asarray(sizes, jnp.int32))

    sizes = jnp.where(number % 4 == 0, named(crowded, number // 4), named(ordinary, number - number // 4 - 1))
    mixed = jax.random.permutation(jax.random.fold_in(own, 3), count)
    source_of, sink = mixed[0:count // 2 * 2:2], mixed[1:count // 2 * 2:2]
    margin = jnp.minimum(sizes[source_of] - 1, most - sizes[sink]) // 2
    margin = jnp.where((source_of == ranking[0]) | (sink == ranking[0]) | (sizes[sink] == 0), 0, jnp.maximum(margin, 0))
    moved = jax.random.randint(jax.random.fold_in(own, 4), (count // 2,), 0, 1 << 20) % (margin + 1)
    sizes = sizes.at[source_of].add(-moved).at[sink].add(moved)
    items = jnp.searchsorted(jnp.cumsum(sizes), jnp.arange(rows * top), side="right").astype(jnp.int32)
    grid = items.reshape(top, rows).T
    grid = grid[jax.random.permutation(jax.random.fold_in(own, 1), rows)]
    turn = jax.random.randint(jax.random.fold_in(own, 2), (rows, 1), 0, top)
    return jnp.take_along_axis(grid, (jnp.arange(top)[None, :] + turn) % top, axis=1)


def shares(number_of, total, reach, skew, full):
    weights = [(1 << 20) // math.isqrt(rank ** skew) + 1 for rank in range(1, number_of + 1)]
    largest = reach if full else min(reach, max(-(-total // number_of), total * weights[0] // sum(weights)))
    least = 1 if total - largest >= number_of - 1 else 0
    counts, rest = [largest] + [least] * (number_of - 1), total - largest - least * (number_of - 1)
    while rest > 0:
        candidates = [i for i in range(1, number_of) if counts[i] < largest] or [i for i in range(1, number_of) if counts[i] < reach]
        pool, remaining = sum([weights[i] for i in candidates]), rest
        for i in candidates:
            extra = min(reach - counts[i], max(1, remaining * weights[i] // pool), rest)
            counts[i] = counts[i] + extra
            rest = rest - extra
    return np.array(counts)


def bell_draw(key, dims, spread, bound, shards=(), held_as=jnp.bfloat16):
    values = spread * jax.random.normal(key, dims, jnp.float32)
    if shards:
        values = values * block_scale(key, dims, shards, -0.22, 0.18)
    return jnp.clip(values, -bound, bound).astype(held_as)


def setup_inputs(seed: int = 0) -> dict:
    splits = jax.random.split(jax.random.key(seed), 5)
    fields = bell_draw(splits[0], (5, NX, NY, NZ), 1.0, 4.0, ((1, 8), (2, 4), (3, 8)), jnp.float32)
    tracer_ref = jnp.clip(jax.random.uniform(splits[1], (3, TRACERS), jnp.float32, -1.0, 1.0) * block_scale(splits[1], (3, TRACERS), ((1, 256),), -0.4, 0.0), -1.0, 1.0)
    host_element = place_ends(jax.random.randint(splits[2], (TRACERS,), 0, EX * EY * EZ), jax.random.fold_in(splits[2], 1), 0, (EX * EY * EZ) - 1).astype(jnp.int32)
    block_owner_keys = jax.random.split(jax.random.fold_in(splits[3], 1), BLOCKS // NB)
    block_owner_turns = jax.random.permutation(jax.random.fold_in(splits[3], 3), BLOCKS // NB)
    block_owner = jax.vmap(lambda own, number: assign_block(jax.random.fold_in(splits[3], 2), own, number, NB, N_GY * N_GZ, 1, CAP, 2))(block_owner_keys, block_owner_turns).reshape((BLOCKS, 1))
    return dict(fields=fields, tracer_ref=tracer_ref, host_element=host_element, block_owner=block_owner)


time_step = 0.01
lift_factor = 14.0
advance_factor = 0.5


def gll_nodes():
    return np.array([-1.0, -0.8717401485096066, -0.5917001814331423, -0.2092992179024789, 0.2092992179024789, 0.5917001814331423, 0.8717401485096066, 1.0])


def legendre_seven(value):
    lower = 1.0
    upper = value
    for order in range(1, 7):
        lower, upper = upper, ((2 * order + 1) * value * upper - order * lower) / (order + 1)
    return upper


def derivative_matrix():
    points = gll_nodes()
    legendre_at = [legendre_seven(float(points[i])) for i in range(8)]
    matrix = np.zeros((8, 8))
    for i in range(8):
        for m in range(8):
            if i != m:
                matrix[i, m] = legendre_at[i] / (legendre_at[m] * (points[i] - points[m]))
    matrix[0, 0] = -14.0
    matrix[7, 7] = 14.0
    return matrix


def lagrange_rows(coordinate):
    points = gll_nodes()
    result = []
    for i in range(8):
        denominator = 1.0
        weight = jnp.ones_like(coordinate)
        for m in range(8):
            if m != i:
                denominator = denominator * (points[i] - points[m])
                weight = weight * (coordinate - float(points[m]))
        result.append(weight * float(1.0 / denominator))
    return jnp.stack(result)


def tensor_weights(coords):
    along_x = lagrange_rows(coords[0])
    along_y = lagrange_rows(coords[1])
    along_z = lagrange_rows(coords[2])
    return (along_x[:, None, None, :] * along_y[None, :, None, :] * along_z[None, None, :, :]).reshape(512, -1)


def derivative(state, direction):
    extent = state.shape
    matrix = jnp.asarray(derivative_matrix(), jnp.float32)
    highest = lax.Precision.HIGHEST
    if direction == 1:
        shaped = state.reshape(extent[0], extent[1] // 8, 8, extent[2] * extent[3])
        result = jnp.einsum('mi,feip->femp', matrix, shaped, precision=highest)
    elif direction == 2:
        shaped = state.reshape(extent[0], extent[1], extent[2] // 8, 8, extent[3])
        result = jnp.einsum('mi,fxeiz->fxemz', matrix, shaped, precision=highest)
    else:
        shaped = state.reshape(extent[0], extent[1], extent[2], extent[3] // 8, 8)
        result = jnp.einsum('mi,fxyei->fxyem', matrix, shaped, precision=highest)
    return result.reshape(extent)


def shifted(scalar, direction):
    if direction == 3:
        return jnp.roll(scalar, 1, 3), jnp.roll(scalar, -1, 3)
    edge = lax.slice_in_dim(jnp.zeros_like(scalar), 0, 1, axis=direction)
    number = scalar.shape[direction]
    lower = lax.slice_in_dim(scalar, 0, number - 1, axis=direction)
    upper = lax.slice_in_dim(scalar, 1, number, axis=direction)
    return jnp.concatenate([edge, lower], direction), jnp.concatenate([upper, edge], direction)


def substep(state):
    velocity = state[0:3]
    pieces = []
    for f in range(5):
        scalar = state[f:f + 1]
        accumulated = jnp.zeros_like(scalar)
        for d in range(3):
            previous, following = shifted(scalar, d + 1)
            gradient = derivative(scalar, d + 1)
            position = lax.broadcasted_iota(jnp.int32, scalar.shape, d + 1) % 8
            face_jump = jnp.where(position == 0, previous - scalar, 0.0) + jnp.where(position == 7, scalar - following, 0.0)
            accumulated = accumulated + velocity[d][None] * (lift_factor * face_jump - gradient)
        pieces.append(scalar + time_step * accumulated)
    return jnp.concatenate(pieces, 0)


def reference(fields, tracer_ref, host_element, block_owner):
    half_step = substep(fields)
    fields_out = substep(half_step)
    element_table = half_step[0:3].astype(jnp.bfloat16).reshape(3, NX // 8, 8, NY // 8, 8, NZ // 8, 8)
    element_table = element_table.transpose(1, 3, 5, 0, 2, 4, 6).reshape(-1, 1536)
    tracer_index = jnp.arange(TRACERS, dtype=jnp.int32)
    device = tracer_index // (NB * 128)
    slab = device // (N_GY * N_GZ)
    owners = jnp.repeat(block_owner[:, 0], 128)
    owner_y = owners // N_GZ
    owner_z = owners % N_GZ
    elem_x = host_element // (EY * EZ)
    elem_y = (host_element // EZ) % EY
    elem_z = host_element % EZ
    global_element = ((slab * EX + elem_x) * (NY // 8) + owner_y * EY + elem_y) * (NZ // 8) + owner_z * EZ + elem_z
    global_element = global_element.astype(jnp.int32)

    def block_velocity(inputs):
        indices, coords = inputs
        gathered = jnp.take(element_table, indices, axis=0).astype(jnp.float32).reshape(-1, 3, 512)
        weights = tensor_weights(coords)
        return jnp.einsum('ncp,pn->cn', gathered, weights, precision=lax.Precision.HIGHEST)

    velocity = lax.map(block_velocity, (global_element.reshape(-1, 2048), tracer_ref.reshape(3, -1, 2048).transpose(1, 0, 2)))
    tracer_velocity = velocity.transpose(1, 0, 2).reshape(3, TRACERS)
    moved_ref = tracer_ref + advance_factor * tracer_velocity
    return fields_out, moved_ref
```

```python
import functools

import jax
import jax.numpy as jnp
import numpy as np
from jax import lax
from jax.experimental import pallas as pl
from jax.experimental.pallas import tpu as pltpu
from jax.sharding import PartitionSpec as P

TIME_STEP = 0.01
LIFT = 14.0
ADVANCE = 0.5
F32 = jnp.float32
BF16 = jnp.bfloat16
MESH = pl.DeviceIdType.MESH


def gll_nodes():
    return np.array(
        [
            -1.0,
            -0.8717401485096066,
            -0.5917001814331423,
            -0.2092992179024789,
            0.2092992179024789,
            0.5917001814331423,
            0.8717401485096066,
            1.0,
        ]
    )


def legendre_seven(value):
    lower = 1.0
    upper = value
    for order in range(1, 7):
        lower, upper = (upper, ((2 * order + 1) * value * upper - order * lower) / (order + 1))
    return upper


def derivative_matrix():
    points = gll_nodes()
    legendre_at = [legendre_seven(float(points[i])) for i in range(8)]
    matrix = np.zeros((8, 8))
    for i in range(8):
        for m in range(8):
            if i != m:
                matrix[i, m] = legendre_at[i] / (legendre_at[m] * (points[i] - points[m]))
    matrix[0, 0] = -14.0
    matrix[7, 7] = 14.0
    return matrix


def split(matrix):
    high = np.asarray(matrix, np.float32).astype(BF16)
    low = (np.asarray(matrix, np.float64) - high.astype(np.float64)).astype(np.float32).astype(BF16)
    return high, low


def constants():
    element = -derivative_matrix()
    element[0, 0] -= LIFT
    element[7, 7] += LIFT
    element = element * TIME_STEP
    eye = np.eye(8)
    both = np.concatenate([np.kron(element, eye), np.kron(eye, element)], 0)
    high, low = split(both)
    planes = np.concatenate([high, high, low], 1)
    line = np.kron(np.eye(16), element)
    for e in range(1, 16):
        line[8 * e, 8 * e - 1] = LIFT * TIME_STEP
        line[8 * e - 1, 8 * e] = -LIFT * TIME_STEP
    high, low = split(line.T)
    line = np.concatenate(
        [
            np.concatenate([high, low], 1),
            np.concatenate([high, np.zeros_like(low)], 1),
        ],
        0,
    )
    points = gll_nodes()
    rows = np.zeros((8, 8))
    for n in range(8):
        others = [points[m] for m in range(8) if m != n]
        rows[:7, n] = others
        rows[7, n] = 1.0 / np.prod([points[n] - other for other in others])
    nodes = np.broadcast_to(rows[:, :, None], (8, 8, 128)).astype(np.float32)
    return planes, line, nodes


def halves(value):
    high = value.astype(BF16)
    low = (value - high.astype(F32)).astype(BF16)
    return high, low


def dot(a, b):
    return jnp.dot(a, b, preferred_element_type=F32)


def body(
    sizes,
    fields_hbm,
    tracer_hbm,
    host_hbm,
    owner_hbm,
    planes_hbm,
    line_hbm,
    nodes_hbm,
    final_hbm,
    moved_hbm,
    state,
    half,
    part,
    final,
    tracer,
    host,
    owner,
    planes,
    line,
    nodes,
    y_out,
    z_out,
    x_in,
    y_in,
    z_in,
    payload,
    unpack,
    outgoing,
    received,
    z_weights,
    xy_weights,
    velocity,
    returned,
    own_velocity,
    moved,
    load_sem,
    halo_send,
    halo_recv,
    route_send,
    route_recv,
    own_sem,
    store_sem,
):
    n_gx, n_gy, n_gz, blocks = sizes
    group = n_gy * n_gz
    gx, gy, gz = lax.axis_index("gx"), lax.axis_index("gy"), lax.axis_index("gz")
    me = gy * n_gz + gz

    loads = [
        pltpu.make_async_copy(source, target, load_sem.at[i])
        for i, (source, target) in enumerate(
            [
                (fields_hbm, state),
                (owner_hbm, owner),
                (tracer_hbm, tracer),
                (host_hbm, host),
                (planes_hbm, planes),
                (line_hbm, line),
                (nodes_hbm, nodes),
            ]
        )
    ]
    for load in loads:
        load.start()

    def peer(k):
        to_y = lax.rem(gy + k // n_gz, n_gy)
        to_z = lax.rem(gz + lax.rem(k, n_gz), n_gz)
        return to_y, to_z

    barrier = pltpu.get_barrier_semaphore()

    def greet(k, carry):
        to_y, to_z = peer(k)
        pl.semaphore_signal(barrier, inc=1, device_id=(gx, to_y, to_z), device_id_type=MESH)
        return carry

    x_low, x_high = lax.rem(gx + n_gx - 1, n_gx), lax.rem(gx + 1, n_gx)
    y_low, y_high = lax.rem(gy + n_gy - 1, n_gy), lax.rem(gy + 1, n_gy)
    z_low, z_high = lax.rem(gz + n_gz - 1, n_gz), lax.rem(gz + 1, n_gz)
    for x in (x_low, x_high):
        pl.semaphore_signal(barrier, inc=1, device_id=(x, gy, gz), device_id_type=MESH)
    lax.fori_loop(1, group, greet, 0)

    lane = lax.broadcasted_iota(jnp.int32, (8, 128), 1)
    sub = lax.broadcasted_iota(jnp.int32, (8, 128), 0)

    def fill_halos(source, step):
        for f in range(5):
            y_out[step, 0, f] = source[f, :, 0, :]
            y_out[step, 1, f] = source[f, :, 7, :]
        packed = jnp.zeros((8, 128), F32)
        for f in range(5):
            for x in range(8):
                at = f * 8 + x
                packed = jnp.where(
                    lane // 2 == at, pltpu.roll(source[f, x], (1 + 2 * at) % 128, 1), packed
                )
        z_out[step] = packed

    def halo_copies(source, step):
        sides = [
            (source.at[:, 0], x_in.at[step, 1], (x_low, gy, gz)),
            (source.at[:, 7], x_in.at[step, 0], (x_high, gy, gz)),
            (y_out.at[step, 0], y_in.at[step, 1], (gx, y_low, gz)),
            (y_out.at[step, 1], y_in.at[step, 0], (gx, y_high, gz)),
            (z_out.at[step], z_in.at[step, 1], (gx, gy, z_low)),
            (z_out.at[step], z_in.at[step, 0], (gx, gy, z_high)),
        ]
        return [
            pltpu.make_async_remote_copy(
                src_ref=source_ref,
                dst_ref=target_ref,
                send_sem=halo_send.at[step, i],
                recv_sem=halo_recv.at[step, i],
                device_id=device,
                device_id_type=MESH,
            )
            for i, (source_ref, target_ref, device) in enumerate(sides)
        ]

    def inner(source):
        wind = [source[d].reshape(64, 128) for d in range(3)]
        for f in range(5):
            value = source[f].reshape(64, 128)
            high, low = halves(value)
            across = dot(planes[...], jnp.concatenate([high, low, high], 0))
            along = dot(jnp.concatenate([high, low], 1), line[...])
            total = value + wind[0] * across[:64] + wind[1] * across[64:]
            total = total + wind[2] * (along[:, :128] + along[:, 128:])
            part[f] = total.reshape(8, 8, 128)

    lift = LIFT * TIME_STEP
    x_prev = jnp.where(gx == 0, 0.0, lift)
    x_next = jnp.where(gx == n_gx - 1, 0.0, -lift)
    y_prev = jnp.where(sub == 0, jnp.where(gy == 0, 0.0, lift), 0.0)
    y_next = jnp.where(sub == 7, jnp.where(gy == n_gy - 1, 0.0, -lift), 0.0)
    z_side = jnp.where(lane == 0, lift, 0.0) + jnp.where(lane == 127, -lift, 0.0)

    def outer(source, target, step):
        merged = jnp.where(
            lane % 2 == 0,
            pltpu.roll(z_in[step, 1], 127, 1),
            pltpu.roll(z_in[step, 0], 1, 1),
        )
        for x in range(8):
            wind = [source[d, x] for d in range(3)]
            y_wind = (wind[1] * y_prev, wind[1] * y_next)
            z_wind = wind[2] * z_side
            for f in range(5):
                at = f * 8 + x
                total = part[f, x]
                if x == 0:
                    total = total + wind[0] * (x_prev * x_in[step, 0, f])
                if x == 7:
                    total = total + wind[0] * (x_next * x_in[step, 1, f])
                total = total + y_wind[0] * y_in[step, 0, f, pl.ds(x, 1), :]
                total = total + y_wind[1] * y_in[step, 1, f, pl.ds(x, 1), :]
                total = total + z_wind * pltpu.roll(merged, (127 - 2 * at) % 128, 1)
                target[f, x] = total

    for load in loads[1:4]:
        load.wait()
    owner_column = jnp.broadcast_to(owner[...].astype(F32), (blocks, 128))
    row = lax.broadcasted_iota(jnp.int32, (blocks, 128), 0)
    column = lax.broadcasted_iota(jnp.int32, (blocks, 128), 1)
    block_lane = lax.rem(column, blocks)
    owner_lane = jnp.sum(jnp.where(row == block_lane, owner_column, 0.0), axis=0, keepdims=True)
    same = owner_column == owner_lane
    earlier_lane = jnp.sum(
        jnp.where(same & (row < block_lane), 1.0, 0.0), axis=0, keepdims=True
    )
    earlier_column = jnp.sum(
        jnp.where(same & (column < row), 1.0, 0.0), axis=1, keepdims=True
    )
    slot_lane = owner_lane * 8.0 + earlier_lane * 4.0
    slot_column = owner_column[:, :1] * 8.0 + earlier_column * 4.0
    for c in range(3):
        wide = lax.broadcasted_iota(jnp.int32, (blocks, group * 8), 1).astype(F32)
        unpack[c * blocks : (c + 1) * blocks, :] = jnp.where(
            wide == slot_column + float(c), 1.0, 0.0
        ).astype(BF16)
    for b in range(blocks):
        payload[pl.ds(b, 3, stride=blocks), :] = tracer[:, b * 128 : (b + 1) * 128]
    payload[3 * blocks :, :] = host[...].astype(F32)
    width = 4 * blocks
    tall = lax.broadcasted_iota(jnp.int32, (group * 8, width), 0).astype(F32)
    part_lane = lax.broadcasted_iota(jnp.int32, (1, width), 1) // blocks
    target_row = slot_lane[:, :width] + part_lane.astype(F32)
    place = jnp.where(tall == target_row, 1.0, 0.0).astype(BF16)
    high, low = halves(payload[...])
    packed = dot(
        jnp.concatenate([place, place], 1), jnp.concatenate([high, low], 0)
    )
    outgoing[...] = packed.reshape(group, 8, 128)

    loads[0].wait()
    fill_halos(state, 0)

    pl.semaphore_wait(barrier, group + 1)

    first = halo_copies(state, 0)
    for copy in first:
        copy.start()

    def send_block(k, carry):
        to_y, to_z = peer(k)
        pltpu.make_async_remote_copy(
            src_ref=outgoing.at[to_y * n_gz + to_z],
            dst_ref=received.at[me],
            send_sem=route_send.at[0],
            recv_sem=route_recv.at[0],
            device_id=(gx, to_y, to_z),
            device_id_type=MESH,
        ).start()
        return carry

    lax.fori_loop(1, group, send_block, 0)
    mine = pltpu.make_async_copy(outgoing.at[me], received.at[me], own_sem.at[0])
    mine.start()

    loads[4].wait()
    loads[5].wait()
    inner(state)
    for copy in first:
        copy.wait_recv()
    outer(state, half, 0)
    fill_halos(half, 1)
    second = halo_copies(half, 1)
    for copy in second:
        copy.start()

    loads[6].wait()
    mine.wait()
    others = received.at[pl.ds(0, group - 1)]
    pltpu.make_async_copy(others, others, route_recv.at[0]).wait()

    def lagrange(coordinate):
        value = nodes[7]
        for k in range(7):
            value = value * (coordinate - nodes[k])
        return value

    def weigh(s, carry):
        for a in range(2):
            lanes = slice(a * 128, (a + 1) * 128)
            coordinate = [received[s, 4 * a + c : 4 * a + c + 1, :] for c in range(4)]
            along = [lagrange(coordinate[c]) for c in range(3)]
            for e in range(16):
                z_weights[s, e * 8 : (e + 1) * 8, lanes] = jnp.where(
                    coordinate[3] == float(e), along[2], 0.0
                ).astype(BF16)
            for i in range(8):
                xy_weights[s, i * 8 : (i + 1) * 8, lanes] = along[0][i : i + 1, :] * along[1]
        return carry

    lax.fori_loop(0, group, weigh, 0)

    table = half[0:3].reshape(192, 128).astype(BF16)

    def interpolate(s):
        values = dot(table, z_weights[s])
        for a in range(2):
            lanes = slice(a * 128, (a + 1) * 128)
            weights = xy_weights[s, :, lanes]
            rows = [
                jnp.sum(values[c * 64 : (c + 1) * 64, lanes] * weights, axis=0, keepdims=True)
                for c in range(3)
            ]
            velocity[s, 4 * a : 4 * a + 4, :] = jnp.concatenate(rows + [jnp.zeros_like(rows[0])], 0)

    def send_back(k, carry):
        to_y, to_z = peer(k)
        s = to_y * n_gz + to_z
        interpolate(s)
        pltpu.make_async_remote_copy(
            src_ref=velocity.at[s],
            dst_ref=returned.at[me],
            send_sem=route_send.at[1],
            recv_sem=route_recv.at[1],
            device_id=(gx, to_y, to_z),
            device_id_type=MESH,
        ).start()
        return carry

    lax.fori_loop(1, group, send_back, 0)
    interpolate(me)
    back = pltpu.make_async_copy(velocity.at[me], returned.at[me], own_sem.at[1])
    back.start()

    inner(half)
    for copy in second:
        copy.wait_recv()
    outer(half, final, 1)
    store = pltpu.make_async_copy(final, final_hbm, store_sem.at[0])
    store.start()

    back.wait()
    others = returned.at[pl.ds(0, group - 1)]
    pltpu.make_async_copy(others, others, route_recv.at[1]).wait()
    high, low = halves(returned[...].reshape(group * 8, 128))
    own_velocity[...] = dot(unpack[...], high) + dot(unpack[...], low)
    for b in range(blocks):
        lanes = slice(b * 128, (b + 1) * 128)
        moved[:, lanes] = (
            tracer[:, lanes] + ADVANCE * own_velocity[pl.ds(b, 3, stride=blocks), :]
        )
    store_moved = pltpu.make_async_copy(moved, moved_hbm, store_sem.at[1])
    store_moved.start()

    for copy in first + second:
        copy.wait_send()
    others = outgoing.at[pl.ds(0, group - 1)]
    pltpu.make_async_copy(others, others, route_send.at[0]).wait()
    others = velocity.at[pl.ds(0, group - 1)]
    pltpu.make_async_copy(others, others, route_send.at[1]).wait()
    store.wait()
    store_moved.wait()


def shards(sizes, fields, tracer_ref, host_element, block_owner):
    n_gx, n_gy, n_gz = sizes
    group = n_gy * n_gz
    blocks = block_owner.shape[0]
    planes, line, nodes = constants()
    any_space = pl.BlockSpec(memory_space=pl.ANY)
    return pl.pallas_call(
        functools.partial(body, (n_gx, n_gy, n_gz, blocks)),
        out_shape=(
            jax.ShapeDtypeStruct(fields.shape, F32),
            jax.ShapeDtypeStruct(tracer_ref.shape, F32),
        ),
        in_specs=[any_space] * 7,
        out_specs=(any_space, any_space),
        scratch_shapes=[
            pltpu.VMEM(fields.shape, F32),
            pltpu.VMEM(fields.shape, F32),
            pltpu.VMEM(fields.shape, F32),
            pltpu.VMEM(fields.shape, F32),
            pltpu.VMEM(tracer_ref.shape, F32),
            pltpu.VMEM((blocks, 128), jnp.int32),
            pltpu.VMEM((blocks, 1), jnp.int32),
            pltpu.VMEM(planes.shape, BF16),
            pltpu.VMEM(line.shape, BF16),
            pltpu.VMEM(nodes.shape, F32),
            pltpu.VMEM((2, 2, 5, 8, 128), F32),
            pltpu.VMEM((2, 8, 128), F32),
            pltpu.VMEM((2, 2, 5, 8, 128), F32),
            pltpu.VMEM((2, 2, 5, 8, 128), F32),
            pltpu.VMEM((2, 2, 8, 128), F32),
            pltpu.VMEM((4 * blocks, 128), F32),
            pltpu.VMEM((3 * blocks, 8 * group), BF16),
            pltpu.VMEM((group, 8, 128), F32),
            pltpu.VMEM((group, 8, 128), F32),
            pltpu.VMEM((group, 128, 256), BF16),
            pltpu.VMEM((group, 64, 256), F32),
            pltpu.VMEM((group, 8, 128), F32),
            pltpu.VMEM((group, 8, 128), F32),
            pltpu.VMEM((3 * blocks, 128), F32),
            pltpu.VMEM(tracer_ref.shape, F32),
            pltpu.SemaphoreType.DMA((7,)),
            pltpu.SemaphoreType.DMA((2, 6)),
            pltpu.SemaphoreType.DMA((2, 6)),
            pltpu.SemaphoreType.DMA((2,)),
            pltpu.SemaphoreType.DMA((2,)),
            pltpu.SemaphoreType.DMA((2,)),
            pltpu.SemaphoreType.DMA((2,)),
        ],
        compiler_params=pltpu.CompilerParams(
            collective_id=0, has_side_effects=True, vmem_limit_bytes=40 * 1024 * 1024
        ),
    )(
        fields,
        tracer_ref,
        host_element.reshape(blocks, 128),
        block_owner,
        jnp.asarray(planes),
        jnp.asarray(line),
        jnp.asarray(nodes),
    )


def solution(mesh):
    sizes = tuple(mesh.shape[axis] for axis in ("gx", "gy", "gz"))
    return jax.shard_map(
        functools.partial(shards, sizes),
        mesh=mesh,
        in_specs=(
            P(None, "gx", "gy", "gz"),
            P(None, ("gx", "gy", "gz")),
            P(("gx", "gy", "gz")),
            P(("gx", "gy", "gz"), None),
        ),
        out_specs=(P(None, "gx", "gy", "gz"), P(None, ("gx", "gy", "gz"))),
        check_vma=False,
    )
```

```python
import functools

import jax
import jax.numpy as jnp
import numpy as np
from jax import lax
from jax.experimental import pallas as pl
from jax.experimental.pallas import tpu as pltpu
from jax.sharding import PartitionSpec as P

TIME_STEP = 0.01
LIFT = 14.0
ADVANCE = 0.5
F32 = jnp.float32
BF16 = jnp.bfloat16
MESH = pl.DeviceIdType.MESH


def gll_nodes():
    return np.array(
        [
            -1.0,
            -0.8717401485096066,
            -0.5917001814331423,
            -0.2092992179024789,
            0.2092992179024789,
            0.5917001814331423,
            0.8717401485096066,
            1.0,
        ]
    )


def legendre_seven(value):
    lower = 1.0
    upper = value
    for order in range(1, 7):
        lower, upper = (upper, ((2 * order + 1) * value * upper - order * lower) / (order + 1))
    return upper


def derivative_matrix():
    points = gll_nodes()
    legendre_at = [legendre_seven(float(points[i])) for i in range(8)]
    matrix = np.zeros((8, 8))
    for i in range(8):
        for m in range(8):
            if i != m:
                matrix[i, m] = legendre_at[i] / (legendre_at[m] * (points[i] - points[m]))
    matrix[0, 0] = -14.0
    matrix[7, 7] = 14.0
    return matrix


def constants():
    element = -derivative_matrix()
    element[0, 0] -= LIFT
    element[7, 7] += LIFT
    element = element * TIME_STEP
    eye = np.eye(8)
    planes = np.concatenate([np.kron(element, eye), np.kron(eye, element)], 0)
    line = np.kron(np.eye(16), element)
    for e in range(1, 16):
        line[8 * e, 8 * e - 1] = LIFT * TIME_STEP
        line[8 * e - 1, 8 * e] = -LIFT * TIME_STEP
    line = line.T
    points = gll_nodes()
    rows = np.zeros((8, 8))
    for n in range(8):
        others = [points[m] for m in range(8) if m != n]
        rows[:7, n] = others
        rows[7, n] = 1.0 / np.prod([points[n] - other for other in others])
    nodes = np.broadcast_to(rows[:, :, None], (8, 8, 128)).astype(np.float32)
    return planes.astype(np.float32), line.astype(np.float32), nodes


def slab_offsets(rows, chips):
    def distance(offset):
        dy, dc, _ = offset
        return min(dy, rows - dy) + min(dc, chips - dc)

    offsets = sorted(
        [(dy, dc, cx) for dy in range(rows) for dc in range(chips) for cx in range(2)],
        key=lambda offset: (distance(offset),) + offset,
    )
    opposite = [offsets.index(((rows - dy) % rows, (chips - dc) % chips, cx)) for dy, dc, cx in offsets]
    rings = [
        [k for k, offset in enumerate(offsets) if distance(offset) == d]
        for d in range(distance(offsets[-1]) + 1)
    ]
    return offsets, opposite, rings


def halves(value):
    high = value.astype(BF16)
    low = (value - high.astype(F32)).astype(BF16)
    return high, low


def dot(a, b):
    return jnp.dot(a, b, preferred_element_type=F32)


def body(
    sizes,
    fields_hbm,
    tracer_hbm,
    host_hbm,
    owner_hbm,
    planes_hbm,
    line_hbm,
    nodes_hbm,
    final,
    moved,
    state,
    half,
    part,
    tracer,
    host,
    owner,
    planes_f32,
    line_f32,
    nodes,
    planes,
    line,
    y_out,
    z_out,
    x_in,
    y_in,
    z_in,
    payload,
    unpack,
    outgoing,
    received,
    z_weights,
    xy_weights,
    velocity,
    returned,
    own_velocity,
    load_sem,
    halo_send,
    halo_recv,
    route_send,
    route_recv,
):
    n_gx, n_gy, n_gz, blocks = sizes
    group = n_gy * n_gz
    gx, gy, gz = lax.axis_index("gx"), lax.axis_index("gy"), lax.axis_index("gz")
    me = gy * n_gz + gz
    offsets, opposite, rings = slab_offsets(n_gy, n_gz // 2)

    loads = [
        pltpu.make_async_copy(source, target, load_sem.at[i])
        for i, (source, target) in enumerate(
            [
                (fields_hbm, state),
                (owner_hbm, owner),
                (tracer_hbm, tracer),
                (host_hbm, host),
                (planes_hbm, planes_f32),
                (line_hbm, line_f32),
                (nodes_hbm, nodes),
            ]
        )
    ]
    for load in loads:
        load.start()

    chip, core = lax.div(gz, 2), lax.rem(gz, 2)
    rows_to = [gy] + [lax.rem(gy + dy, n_gy) for dy in range(1, n_gy)]
    chips_to = [chip] + [lax.rem(chip + dc, n_gz // 2) for dc in range(1, n_gz // 2)]
    cores_to = [core, 1 - core]

    def peer(k):
        dy, dc, cx = offsets[k]
        return rows_to[dy], chips_to[dc] * 2 + cores_to[cx]

    x_low, x_high = lax.rem(gx + n_gx - 1, n_gx), lax.rem(gx + 1, n_gx)
    y_low, y_high = lax.rem(gy + n_gy - 1, n_gy), lax.rem(gy + 1, n_gy)
    z_low, z_high = lax.rem(gz + n_gz - 1, n_gz), lax.rem(gz + 1, n_gz)

    barrier = pltpu.get_barrier_semaphore()
    for k in range(group - 1, 0, -1):
        pl.semaphore_signal(barrier, inc=1, device_id=(gx,) + peer(k), device_id_type=MESH)
    for x in (x_low, x_high):
        pl.semaphore_signal(barrier, inc=1, device_id=(x, gy, gz), device_id_type=MESH)

    lane = lax.broadcasted_iota(jnp.int32, (8, 128), 1)
    sub = lax.broadcasted_iota(jnp.int32, (8, 128), 0)

    def fill_halos(source, step):
        for f in range(5):
            y_out[step, 0, f] = source[f, :, 0, :]
            y_out[step, 1, f] = source[f, :, 7, :]
        packed = jnp.zeros((8, 128), F32)
        for f in range(5):
            for x in range(8):
                at = f * 8 + x
                packed = jnp.where(
                    lane // 2 == at, pltpu.roll(source[f, x], (1 + 2 * at) % 128, 1), packed
                )
        z_out[step] = packed

    def halo_copies(source, step):
        sides = [
            (source.at[:, 0], x_in.at[step, 1], (x_low, gy, gz)),
            (source.at[:, 7], x_in.at[step, 0], (x_high, gy, gz)),
            (y_out.at[step, 0], y_in.at[step, 1], (gx, y_low, gz)),
            (y_out.at[step, 1], y_in.at[step, 0], (gx, y_high, gz)),
            (z_out.at[step], z_in.at[step, 1], (gx, gy, z_low)),
            (z_out.at[step], z_in.at[step, 0], (gx, gy, z_high)),
        ]
        return [
            pltpu.make_async_remote_copy(
                src_ref=source_ref,
                dst_ref=target_ref,
                send_sem=halo_send.at[step, i],
                recv_sem=halo_recv.at[step, i],
                device_id=device,
                device_id_type=MESH,
            )
            for i, (source_ref, target_ref, device) in enumerate(sides)
        ]

    def inner(source):
        wind = [source[d].reshape(64, 128) for d in range(3)]
        for f in range(5):
            value = source[f].reshape(64, 128)
            high, low = halves(value)
            across = dot(planes[...], jnp.concatenate([high, low, high], 0))
            along = dot(jnp.concatenate([high, low], 1), line[...])
            total = value + wind[0] * across[:64] + wind[1] * across[64:]
            total = total + wind[2] * (along[:, :128] + along[:, 128:])
            part[f] = total.reshape(8, 8, 128)

    lift = LIFT * TIME_STEP
    x_prev = jnp.where(gx == 0, 0.0, lift)
    x_next = jnp.where(gx == n_gx - 1, 0.0, -lift)
    y_prev = jnp.where(sub == 0, jnp.where(gy == 0, 0.0, lift), 0.0)
    y_next = jnp.where(sub == 7, jnp.where(gy == n_gy - 1, 0.0, -lift), 0.0)
    z_side = jnp.where(lane == 0, lift, 0.0) + jnp.where(lane == 127, -lift, 0.0)

    def outer(source, target, step):
        merged = jnp.where(
            lane % 2 == 0,
            pltpu.roll(z_in[step, 1], 127, 1),
            pltpu.roll(z_in[step, 0], 1, 1),
        )
        for x in range(8):
            wind = [source[d, x] for d in range(3)]
            y_wind = (wind[1] * y_prev, wind[1] * y_next)
            z_wind = wind[2] * z_side
            for f in range(5):
                at = f * 8 + x
                total = part[f, x]
                if x == 0:
                    total = total + wind[0] * (x_prev * x_in[step, 0, f])
                if x == 7:
                    total = total + wind[0] * (x_next * x_in[step, 1, f])
                total = total + y_wind[0] * y_in[step, 0, f, pl.ds(x, 1), :]
                total = total + y_wind[1] * y_in[step, 1, f, pl.ds(x, 1), :]
                total = total + z_wind * pltpu.roll(merged, (127 - 2 * at) % 128, 1)
                target[f, x] = total

    for load in loads[1:4]:
        load.wait()
    square = jnp.broadcast_to(owner[...].astype(F32), (blocks, blocks))
    diagonal = lax.broadcasted_iota(jnp.int32, (blocks, blocks), 0) == lax.broadcasted_iota(
        jnp.int32, (blocks, blocks), 1
    )
    owner_column = jnp.sum(jnp.where(diagonal, square, 0.0), axis=1, keepdims=True)
    owner_column = jnp.broadcast_to(owner_column, (blocks, 128))
    row = lax.broadcasted_iota(jnp.int32, (blocks, 128), 0)
    column = lax.broadcasted_iota(jnp.int32, (blocks, 128), 1)
    block_lane = lax.rem(column, blocks)
    owner_lane = jnp.sum(jnp.where(row == block_lane, owner_column, 0.0), axis=0, keepdims=True)
    same = owner_column == owner_lane
    earlier_lane = jnp.sum(
        jnp.where(same & (row < block_lane), 1.0, 0.0), axis=0, keepdims=True
    )
    earlier_column = jnp.sum(
        jnp.where(same & (column < row), 1.0, 0.0), axis=1, keepdims=True
    )
    slot_lane = owner_lane * 8.0 + earlier_lane * 4.0
    slot_column = owner_column[:, :1] * 8.0 + earlier_column * 4.0
    for c in range(3):
        wide = lax.broadcasted_iota(jnp.int32, (blocks, group * 8), 1).astype(F32)
        unpack[c * blocks : (c + 1) * blocks, :] = jnp.where(
            wide == slot_column + float(c), 1.0, 0.0
        ).astype(BF16)
    for b in range(blocks):
        payload[pl.ds(b, 3, stride=blocks), :] = tracer[:, b * 128 : (b + 1) * 128]
    payload[3 * blocks :, :] = host[...].astype(F32)
    width = 4 * blocks
    tall = lax.broadcasted_iota(jnp.int32, (group * 8, width), 0).astype(F32)
    part_lane = lax.broadcasted_iota(jnp.int32, (1, width), 1) // blocks
    target_row = slot_lane[:, :width] + part_lane.astype(F32)
    place = jnp.where(tall == target_row, 1.0, 0.0).astype(BF16)
    high, low = halves(payload[...])
    packed = dot(
        jnp.concatenate([place, place], 1), jnp.concatenate([high, low], 0)
    )
    outgoing[...] = packed.reshape(group, 8, 128)

    loads[4].wait()
    loads[5].wait()
    high, low = halves(planes_f32[...])
    planes[...] = jnp.concatenate([high, high, low], 1)
    high, low = halves(line_f32[...])
    line[:128, :128] = high
    line[128:, :128] = high
    line[:128, 128:] = low
    line[128:, 128:] = jnp.zeros_like(low)

    loads[0].wait()
    fill_halos(state, 0)

    pl.semaphore_wait(barrier, group + 1)

    def send_block(k):
        to_y, to_z = peer(k)
        pltpu.make_async_remote_copy(
            src_ref=outgoing.at[to_y * n_gz + to_z],
            dst_ref=received.at[opposite[k]],
            send_sem=route_send.at[0],
            recv_sem=route_recv.at[0, ring_of(k)],
            device_id=(gx, to_y, to_z),
            device_id_type=MESH,
        ).start()

    def ring_of(k):
        return [i for i, ring in enumerate(rings) if k in ring][0]

    far = [k for ring in rings[3:][::-1] for k in ring]
    near = [k for ring in rings[:3][::-1] for k in ring if k > 0]
    for k in far:
        send_block(k)
    first = halo_copies(state, 0)
    for copy in first:
        copy.start()
    for k in near:
        send_block(k)
    received[0] = outgoing[me]

    inner(state)
    for copy in first:
        copy.wait_recv()
    outer(state, half, 0)
    fill_halos(half, 1)
    second = halo_copies(half, 1)
    for copy in second:
        copy.start()

    loads[6].wait()
    table = half[0:3].reshape(192, 128).astype(BF16)
    lower_half = jnp.where(lax.broadcasted_iota(jnp.int32, (16, 128), 0) >= 8, 1.0, 0.0)

    def lagrange(coordinate):
        value = nodes[7]
        for k in range(7):
            value = value * (coordinate - nodes[k])
        return value

    def weigh(s):
        for a in range(2):
            lanes = slice(a * 128, (a + 1) * 128)
            coordinate = [received[s, 4 * a + c : 4 * a + c + 1, :] for c in range(4)]
            along = [lagrange(coordinate[c]) for c in range(3)]
            pair = jnp.concatenate([along[2], along[2]], 0).astype(BF16)
            even = (coordinate[3] - lower_half).astype(BF16)
            for e in range(8):
                z_weights[s, e * 16 : (e + 1) * 16, lanes] = jnp.where(
                    even == jnp.asarray(2 * e, BF16), pair, jnp.zeros_like(pair)
                )
            for i in range(8):
                xy_weights[s, i * 8 : (i + 1) * 8, lanes] = along[0][i : i + 1, :] * along[1]

    def interpolate(s):
        values = dot(table, z_weights[s])
        for a in range(2):
            lanes = slice(a * 128, (a + 1) * 128)
            weights = xy_weights[s, :, lanes]
            rows = [
                jnp.sum(values[c * 64 : (c + 1) * 64, lanes] * weights, axis=0, keepdims=True)
                for c in range(3)
            ]
            velocity[s, 4 * a : 4 * a + 4, :] = jnp.concatenate(rows + [jnp.zeros_like(rows[0])], 0)

    def ring_bytes(ring, buffer):
        return buffer.at[pl.ds(0, len([k for k in ring if k > 0]))]

    def weigh_ring(i):
        ring = rings[i]
        span = ring_bytes(ring, received)
        pltpu.make_async_copy(span, span, route_recv.at[0, i]).wait()

        def step(s, carry):
            weigh(s)
            return carry

        lax.fori_loop(ring[0], ring[-1] + 1, step, 0)

    def answer_ring(i):
        for k in rings[i]:
            interpolate(k)
        for k in rings[i]:
            if k == 0:
                returned[me] = velocity[0]
                continue
            pltpu.make_async_remote_copy(
                src_ref=velocity.at[k],
                dst_ref=returned.at[me],
                send_sem=route_send.at[1],
                recv_sem=route_recv.at[1, 0],
                device_id=(gx,) + peer(k),
                device_id_type=MESH,
            ).start()

    for i in range(len(rings)):
        weigh_ring(i)
    for i in range(len(rings)-1,-1,-1):
        answer_ring(i)

    inner(half)
    for copy in second:
        copy.wait_recv()
    outer(half, final, 1)

    others = returned.at[pl.ds(0, group - 1)]
    pltpu.make_async_copy(others, others, route_recv.at[1, 0]).wait()
    high, low = halves(returned[...].reshape(group * 8, 128))
    own_velocity[...] = dot(unpack[...], high) + dot(unpack[...], low)
    for b in range(blocks):
        lanes = slice(b * 128, (b + 1) * 128)
        moved[:, lanes] = (
            tracer[:, lanes] + ADVANCE * own_velocity[pl.ds(b, 3, stride=blocks), :]
        )

    for copy in first + second:
        copy.wait_send()
    others = outgoing.at[pl.ds(0, group - 1)]
    pltpu.make_async_copy(others, others, route_send.at[0]).wait()
    others = velocity.at[pl.ds(0, group - 1)]
    pltpu.make_async_copy(others, others, route_send.at[1]).wait()


def shards(sizes, fields, tracer_ref, host_element, block_owner):
    n_gx, n_gy, n_gz = sizes
    group = n_gy * n_gz
    blocks = block_owner.shape[0]
    planes, line, nodes = constants()
    arrays = (
        fields,
        tracer_ref,
        host_element.reshape(blocks, 128),
        block_owner.reshape(1, blocks),
        jnp.asarray(planes),
        jnp.asarray(line),
        jnp.asarray(nodes),
    )
    in_hbm = pl.BlockSpec(memory_space=pltpu.HBM)
    in_vmem = pl.BlockSpec(memory_space=pltpu.VMEM)
    return pl.pallas_call(
        functools.partial(body, (n_gx, n_gy, n_gz, blocks)),
        out_shape=(
            jax.ShapeDtypeStruct(fields.shape, F32),
            jax.ShapeDtypeStruct(tracer_ref.shape, F32),
        ),
        in_specs=[in_hbm] * len(arrays),
        out_specs=(in_vmem, in_vmem),
        scratch_shapes=[
            pltpu.VMEM(fields.shape, F32),
            pltpu.VMEM(fields.shape, F32),
            pltpu.VMEM(fields.shape, F32),
            pltpu.VMEM(tracer_ref.shape, F32),
            pltpu.VMEM((blocks, 128), jnp.int32),
            pltpu.VMEM((1, blocks), jnp.int32),
            pltpu.VMEM(planes.shape, F32),
            pltpu.VMEM(line.shape, F32),
            pltpu.VMEM(nodes.shape, F32),
            pltpu.VMEM((128, 192), BF16),
            pltpu.VMEM((256, 256), BF16),
            pltpu.VMEM((2, 2, 5, 8, 128), F32),
            pltpu.VMEM((2, 8, 128), F32),
            pltpu.VMEM((2, 2, 5, 8, 128), F32),
            pltpu.VMEM((2, 2, 5, 8, 128), F32),
            pltpu.VMEM((2, 2, 8, 128), F32),
            pltpu.VMEM((4 * blocks, 128), F32),
            pltpu.VMEM((3 * blocks, 8 * group), BF16),
            pltpu.VMEM((group, 8, 128), F32),
            pltpu.VMEM((group, 8, 128), F32),
            pltpu.VMEM((group, 128, 256), BF16),
            pltpu.VMEM((group, 64, 256), F32),
            pltpu.VMEM((group, 8, 128), F32),
            pltpu.VMEM((group, 8, 128), F32),
            pltpu.VMEM((3 * blocks, 128), F32),
            pltpu.SemaphoreType.DMA((len(arrays),)),
            pltpu.SemaphoreType.DMA((2, 6)),
            pltpu.SemaphoreType.DMA((2, 6)),
            pltpu.SemaphoreType.DMA((2,)),
            pltpu.SemaphoreType.DMA((2, 8)),
        ],
        compiler_params=pltpu.CompilerParams(
            collective_id=0, has_side_effects=True, vmem_limit_bytes=40 * 1024 * 1024
        ),
    )(*[pltpu.with_memory_space_constraint(array, pltpu.HBM) for array in arrays])


def solution(mesh):
    sizes = tuple(mesh.shape[axis] for axis in ("gx", "gy", "gz"))
    return jax.shard_map(
        functools.partial(shards, sizes),
        mesh=mesh,
        in_specs=(
            P(None, "gx", "gy", "gz"),
            P(None, ("gx", "gy", "gz")),
            P(("gx", "gy", "gz")),
            P(("gx", "gy", "gz"), None),
        ),
        out_specs=(P(None, "gx", "gy", "gz"), P(None, ("gx", "gy", "gz"))),
        check_vma=False,
    )
```

```python
import functools

import jax
import jax.numpy as jnp
import numpy as np
from jax import lax
from jax.experimental import pallas as pl
from jax.experimental.pallas import tpu as pltpu
from jax.sharding import PartitionSpec as P

TIME_STEP = 0.01
LIFT = 14.0
ADVANCE = 0.5
F32 = jnp.float32
BF16 = jnp.bfloat16
MESH = pl.DeviceIdType.MESH


def gll_nodes():
    return np.array(
        [
            -1.0,
            -0.8717401485096066,
            -0.5917001814331423,
            -0.2092992179024789,
            0.2092992179024789,
            0.5917001814331423,
            0.8717401485096066,
            1.0,
        ]
    )


def legendre_seven(value):
    lower = 1.0
    upper = value
    for order in range(1, 7):
        lower, upper = (upper, ((2 * order + 1) * value * upper - order * lower) / (order + 1))
    return upper


def derivative_matrix():
    points = gll_nodes()
    legendre_at = [legendre_seven(float(points[i])) for i in range(8)]
    matrix = np.zeros((8, 8))
    for i in range(8):
        for m in range(8):
            if i != m:
                matrix[i, m] = legendre_at[i] / (legendre_at[m] * (points[i] - points[m]))
    matrix[0, 0] = -14.0
    matrix[7, 7] = 14.0
    return matrix


def constants():
    element = -derivative_matrix()
    element[0, 0] -= LIFT
    element[7, 7] += LIFT
    element = element * TIME_STEP
    eye = np.eye(8)
    planes = np.concatenate([np.kron(element, eye), np.kron(eye, element)], 0)
    line = np.kron(np.eye(16), element)
    for e in range(1, 16):
        line[8 * e, 8 * e - 1] = LIFT * TIME_STEP
        line[8 * e - 1, 8 * e] = -LIFT * TIME_STEP
    line = line.T
    points = gll_nodes()
    rows = np.zeros((8, 8))
    for n in range(8):
        others = [points[m] for m in range(8) if m != n]
        rows[:7, n] = others
        rows[7, n] = 1.0 / np.prod([points[n] - other for other in others])
    nodes = np.broadcast_to(rows[:, :, None], (8, 8, 128)).astype(np.float32)
    return planes.astype(np.float32), line.astype(np.float32), nodes


def slab_offsets(rows, chips):
    def distance(offset):
        dy, dc, _ = offset
        return min(dy, rows - dy) + min(dc, chips - dc)

    offsets = sorted(
        [(dy, dc, cx) for dy in range(rows) for dc in range(chips) for cx in range(2)],
        key=lambda offset: (distance(offset),) + offset,
    )
    opposite = [offsets.index(((rows - dy) % rows, (chips - dc) % chips, cx)) for dy, dc, cx in offsets]
    rings = [
        [k for k, offset in enumerate(offsets) if distance(offset) == d]
        for d in range(distance(offsets[-1]) + 1)
    ]
    return offsets, opposite, rings


def halves(value):
    high = value.astype(BF16)
    low = (value - high.astype(F32)).astype(BF16)
    return high, low


def dot(a, b):
    return jnp.dot(a, b, preferred_element_type=F32)


def body(
    sizes,
    fields_hbm,
    tracer_hbm,
    host_hbm,
    owner_hbm,
    planes_hbm,
    line_hbm,
    nodes_hbm,
    final,
    moved,
    state,
    half,
    part,
    tracer,
    host,
    owner,
    planes_f32,
    line_f32,
    nodes,
    planes,
    line,
    y_out,
    z_out,
    x_in,
    y_in,
    z_in,
    payload,
    unpack,
    outgoing,
    received,
    z_weights,
    xy_weights,
    velocity,
    returned,
    own_velocity,
    load_sem,
    halo_send,
    halo_recv,
    route_send,
    route_recv,
):
    n_gx, n_gy, n_gz, blocks = sizes
    group = n_gy * n_gz
    gx, gy, gz = lax.axis_index("gx"), lax.axis_index("gy"), lax.axis_index("gz")
    me = gy * n_gz + gz
    offsets, opposite, rings = slab_offsets(n_gy, n_gz // 2)

    loads = [
        pltpu.make_async_copy(source, target, load_sem.at[i])
        for i, (source, target) in enumerate(
            [
                (fields_hbm, state),
                (owner_hbm, owner),
                (tracer_hbm, tracer),
                (host_hbm, host),
                (planes_hbm, planes_f32),
                (line_hbm, line_f32),
                (nodes_hbm, nodes),
            ]
        )
    ]
    for load in loads:
        load.start()

    chip, core = lax.div(gz, 2), lax.rem(gz, 2)
    rows_to = [gy] + [lax.rem(gy + dy, n_gy) for dy in range(1, n_gy)]
    chips_to = [chip] + [lax.rem(chip + dc, n_gz // 2) for dc in range(1, n_gz // 2)]
    cores_to = [core, 1 - core]

    def peer(k):
        dy, dc, cx = offsets[k]
        return rows_to[dy], chips_to[dc] * 2 + cores_to[cx]

    has_low, has_high = gx > 0, gx < n_gx - 1
    x_low, x_high = jnp.maximum(gx - 1, 0), jnp.minimum(gx + 1, n_gx - 1)
    y_low, y_high = lax.rem(gy + n_gy - 1, n_gy), lax.rem(gy + 1, n_gy)
    z_low, z_high = lax.rem(gz + n_gz - 1, n_gz), lax.rem(gz + 1, n_gz)

    barrier = pltpu.get_barrier_semaphore()
    for k in range(group - 1, 0, -1):
        pl.semaphore_signal(barrier, inc=1, device_id=(gx,) + peer(k), device_id_type=MESH)
    for x, present in ((x_low, has_low), (x_high, has_high)):

        @pl.when(present)
        def _(x=x):
            pl.semaphore_signal(barrier, inc=1, device_id=(x, gy, gz), device_id_type=MESH)

    for side, present in ((0, has_low), (1, has_high)):

        @pl.when(jnp.logical_not(present))
        def _(side=side):
            for step in range(2):
                x_in[step, side] = jnp.zeros_like(x_in[step, side])

    sends_when = [has_low, has_high, None, None, None, None]
    comes_when = [has_high, has_low, None, None, None, None]

    def each(copies, conditions, act):
        for copy, condition in zip(copies, conditions):
            if condition is None:
                act(copy)
            else:
                pl.when(condition)(functools.partial(act, copy))

    def start_halos(copies):
        each(copies, sends_when, lambda copy: copy.start())

    def await_halos(copies):
        each(copies, comes_when, lambda copy: copy.wait_recv())


    lane = lax.broadcasted_iota(jnp.int32, (8, 128), 1)
    sub = lax.broadcasted_iota(jnp.int32, (8, 128), 0)

    def fill_halos(source, step):
        for f in range(5):
            y_out[step, 0, f] = source[f, :, 0, :]
            y_out[step, 1, f] = source[f, :, 7, :]
        packed = jnp.zeros((8, 128), F32)
        for f in range(5):
            for x in range(8):
                at = f * 8 + x
                packed = jnp.where(
                    lane // 2 == at, pltpu.roll(source[f, x], (1 + 2 * at) % 128, 1), packed
                )
        z_out[step] = packed

    def halo_copies(source, step):
        sides = [
            (source.at[:, 0], x_in.at[step, 1], (x_low, gy, gz)),
            (source.at[:, 7], x_in.at[step, 0], (x_high, gy, gz)),
            (y_out.at[step, 0], y_in.at[step, 1], (gx, y_low, gz)),
            (y_out.at[step, 1], y_in.at[step, 0], (gx, y_high, gz)),
            (z_out.at[step], z_in.at[step, 1], (gx, gy, z_low)),
            (z_out.at[step], z_in.at[step, 0], (gx, gy, z_high)),
        ]
        return [
            pltpu.make_async_remote_copy(
                src_ref=source_ref,
                dst_ref=target_ref,
                send_sem=halo_send.at[step, i],
                recv_sem=halo_recv.at[step, i],
                device_id=device,
                device_id_type=MESH,
            )
            for i, (source_ref, target_ref, device) in enumerate(sides)
        ]

    def inner(source):
        wind = [source[d].reshape(64, 128) for d in range(3)]
        for f in range(5):
            value = source[f].reshape(64, 128)
            high, low = halves(value)
            across = dot(planes[...], jnp.concatenate([high, low, high], 0))
            along = dot(jnp.concatenate([high, low], 1), line[...])
            total = value + wind[0] * across[:64] + wind[1] * across[64:]
            total = total + wind[2] * (along[:, :128] + along[:, 128:])
            part[f] = total.reshape(8, 8, 128)

    lift = LIFT * TIME_STEP
    x_prev = jnp.where(gx == 0, 0.0, lift)
    x_next = jnp.where(gx == n_gx - 1, 0.0, -lift)
    y_prev = jnp.where(sub == 0, jnp.where(gy == 0, 0.0, lift), 0.0)
    y_next = jnp.where(sub == 7, jnp.where(gy == n_gy - 1, 0.0, -lift), 0.0)
    z_side = jnp.where(lane == 0, lift, 0.0) + jnp.where(lane == 127, -lift, 0.0)

    def outer(source, target, step):
        merged = jnp.where(
            lane % 2 == 0,
            pltpu.roll(z_in[step, 1], 127, 1),
            pltpu.roll(z_in[step, 0], 1, 1),
        )
        for x in range(8):
            wind = [source[d, x] for d in range(3)]
            y_wind = (wind[1] * y_prev, wind[1] * y_next)
            z_wind = wind[2] * z_side
            for f in range(5):
                at = f * 8 + x
                total = part[f, x]
                if x == 0:
                    total = total + wind[0] * (x_prev * x_in[step, 0, f])
                if x == 7:
                    total = total + wind[0] * (x_next * x_in[step, 1, f])
                total = total + y_wind[0] * y_in[step, 0, f, pl.ds(x, 1), :]
                total = total + y_wind[1] * y_in[step, 1, f, pl.ds(x, 1), :]
                total = total + z_wind * pltpu.roll(merged, (127 - 2 * at) % 128, 1)
                target[f, x] = total

    for load in loads[1:4]:
        load.wait()
    square = jnp.broadcast_to(owner[...].astype(F32), (blocks, blocks))
    diagonal = lax.broadcasted_iota(jnp.int32, (blocks, blocks), 0) == lax.broadcasted_iota(
        jnp.int32, (blocks, blocks), 1
    )
    owner_column = jnp.sum(jnp.where(diagonal, square, 0.0), axis=1, keepdims=True)
    owner_column = jnp.broadcast_to(owner_column, (blocks, 128))
    row = lax.broadcasted_iota(jnp.int32, (blocks, 128), 0)
    column = lax.broadcasted_iota(jnp.int32, (blocks, 128), 1)
    block_lane = lax.rem(column, blocks)
    owner_lane = jnp.sum(jnp.where(row == block_lane, owner_column, 0.0), axis=0, keepdims=True)
    same = owner_column == owner_lane
    earlier_lane = jnp.sum(
        jnp.where(same & (row < block_lane), 1.0, 0.0), axis=0, keepdims=True
    )
    earlier_column = jnp.sum(
        jnp.where(same & (column < row), 1.0, 0.0), axis=1, keepdims=True
    )
    slot_lane = owner_lane * 8.0 + earlier_lane * 4.0
    slot_column = owner_column[:, :1] * 8.0 + earlier_column * 4.0
    for c in range(3):
        wide = lax.broadcasted_iota(jnp.int32, (blocks, group * 8), 1).astype(F32)
        unpack[c * blocks : (c + 1) * blocks, :] = jnp.where(
            wide == slot_column + float(c), 1.0, 0.0
        ).astype(BF16)
    for b in range(blocks):
        payload[pl.ds(b, 3, stride=blocks), :] = tracer[:, b * 128 : (b + 1) * 128]
    payload[3 * blocks :, :] = host[...].astype(F32)
    width = 4 * blocks
    tall = lax.broadcasted_iota(jnp.int32, (group * 8, width), 0).astype(F32)
    part_lane = lax.broadcasted_iota(jnp.int32, (1, width), 1) // blocks
    target_row = slot_lane[:, :width] + part_lane.astype(F32)
    place = jnp.where(tall == target_row, 1.0, 0.0).astype(BF16)
    high, low = halves(payload[...])
    packed = dot(
        jnp.concatenate([place, place], 1), jnp.concatenate([high, low], 0)
    )
    outgoing[...] = packed.reshape(group, 8, 128)

    loads[4].wait()
    loads[5].wait()
    high, low = halves(planes_f32[...])
    planes[...] = jnp.concatenate([high, high, low], 1)
    high, low = halves(line_f32[...])
    line[:128, :128] = high
    line[128:, :128] = high
    line[:128, 128:] = low
    line[128:, 128:] = jnp.zeros_like(low)

    loads[0].wait()
    fill_halos(state, 0)

    pl.semaphore_wait(barrier, group - 1 + has_low.astype(jnp.int32) + has_high.astype(jnp.int32))

    def send_block(k):
        to_y, to_z = peer(k)
        pltpu.make_async_remote_copy(
            src_ref=outgoing.at[to_y * n_gz + to_z],
            dst_ref=received.at[opposite[k]],
            send_sem=route_send.at[0],
            recv_sem=route_recv.at[0, ring_of(k)],
            device_id=(gx, to_y, to_z),
            device_id_type=MESH,
        ).start()

    def ring_of(k):
        return [i for i, ring in enumerate(rings) if k in ring][0]

    far = [k for ring in rings[3:][::-1] for k in ring]
    near = [k for ring in rings[:3][::-1] for k in ring if k > 0]
    for k in far:
        send_block(k)
    first = halo_copies(state, 0)
    start_halos(first)
    for k in near:
        send_block(k)
    received[0] = outgoing[me]

    inner(state)
    await_halos(first)
    outer(state, half, 0)
    fill_halos(half, 1)
    second = halo_copies(half, 1)
    start_halos(second)

    loads[6].wait()
    table = half[0:3].reshape(192, 128).astype(BF16)
    lower_half = jnp.where(lax.broadcasted_iota(jnp.int32, (16, 128), 0) >= 8, 1.0, 0.0)

    def lagrange(coordinate):
        value = nodes[7]
        for k in range(7):
            value = value * (coordinate - nodes[k])
        return value

    def weigh(s):
        for a in range(2):
            lanes = slice(a * 128, (a + 1) * 128)
            coordinate = [received[s, 4 * a + c : 4 * a + c + 1, :] for c in range(4)]
            along = [lagrange(coordinate[c]) for c in range(3)]
            pair = jnp.concatenate([along[2], along[2]], 0).astype(BF16)
            even = (coordinate[3] - lower_half).astype(BF16)
            for e in range(8):
                z_weights[s, e * 16 : (e + 1) * 16, lanes] = jnp.where(
                    even == jnp.asarray(2 * e, BF16), pair, jnp.zeros_like(pair)
                )
            for i in range(8):
                xy_weights[s, i * 8 : (i + 1) * 8, lanes] = along[0][i : i + 1, :] * along[1]

    def interpolate(s):
        values = dot(table, z_weights[s])
        for a in range(2):
            lanes = slice(a * 128, (a + 1) * 128)
            weights = xy_weights[s, :, lanes]
            rows = [
                jnp.sum(values[c * 64 : (c + 1) * 64, lanes] * weights, axis=0, keepdims=True)
                for c in range(3)
            ]
            velocity[s, 4 * a : 4 * a + 4, :] = jnp.concatenate(rows + [jnp.zeros_like(rows[0])], 0)

    def ring_bytes(ring, buffer):
        return buffer.at[pl.ds(0, len([k for k in ring if k > 0]))]

    def weigh_ring(i):
        ring = rings[i]
        span = ring_bytes(ring, received)
        pltpu.make_async_copy(span, span, route_recv.at[0, i]).wait()

        def step(s, carry):
            weigh(s)
            return carry

        lax.fori_loop(ring[0], ring[-1] + 1, step, 0)

    def answer_ring(i):
        for k in rings[i]:
            interpolate(k)
        for k in rings[i]:
            if k == 0:
                returned[me] = velocity[0]
                continue
            pltpu.make_async_remote_copy(
                src_ref=velocity.at[k],
                dst_ref=returned.at[me],
                send_sem=route_send.at[1],
                recv_sem=route_recv.at[1, 0],
                device_id=(gx,) + peer(k),
                device_id_type=MESH,
            ).start()

    last = len(rings) - 1
    for i in [0, 1]:
        weigh_ring(i)
    for i in range(last, 1, -1):
        weigh_ring(i)
        answer_ring(i)
    for i in [1, 0]:
        answer_ring(i)

    inner(half)
    await_halos(second)
    outer(half, final, 1)

    others = returned.at[pl.ds(0, group - 1)]
    pltpu.make_async_copy(others, others, route_recv.at[1, 0]).wait()
    high, low = halves(returned[...].reshape(group * 8, 128))
    own_velocity[...] = dot(unpack[...], high) + dot(unpack[...], low)
    for b in range(blocks):
        lanes = slice(b * 128, (b + 1) * 128)
        moved[:, lanes] = (
            tracer[:, lanes] + ADVANCE * own_velocity[pl.ds(b, 3, stride=blocks), :]
        )

    for copies in (first, second):
        each(copies, sends_when, lambda copy: copy.wait_send())
    others = outgoing.at[pl.ds(0, group - 1)]
    pltpu.make_async_copy(others, others, route_send.at[0]).wait()
    others = velocity.at[pl.ds(0, group - 1)]
    pltpu.make_async_copy(others, others, route_send.at[1]).wait()


def shards(sizes, fields, tracer_ref, host_element, block_owner):
    n_gx, n_gy, n_gz = sizes
    group = n_gy * n_gz
    blocks = block_owner.shape[0]
    planes, line, nodes = constants()
    arrays = (
        fields,
        tracer_ref,
        host_element.reshape(blocks, 128),
        block_owner.reshape(1, blocks),
        jnp.asarray(planes),
        jnp.asarray(line),
        jnp.asarray(nodes),
    )
    in_hbm = pl.BlockSpec(memory_space=pltpu.HBM)
    in_vmem = pl.BlockSpec(memory_space=pltpu.VMEM)
    return pl.pallas_call(
        functools.partial(body, (n_gx, n_gy, n_gz, blocks)),
        out_shape=(
            jax.ShapeDtypeStruct(fields.shape, F32),
            jax.ShapeDtypeStruct(tracer_ref.shape, F32),
        ),
        in_specs=[in_hbm] * len(arrays),
        out_specs=(in_vmem, in_vmem),
        scratch_shapes=[
            pltpu.VMEM(fields.shape, F32),
            pltpu.VMEM(fields.shape, F32),
            pltpu.VMEM(fields.shape, F32),
            pltpu.VMEM(tracer_ref.shape, F32),
            pltpu.VMEM((blocks, 128), jnp.int32),
            pltpu.VMEM((1, blocks), jnp.int32),
            pltpu.VMEM(planes.shape, F32),
            pltpu.VMEM(line.shape, F32),
            pltpu.VMEM(nodes.shape, F32),
            pltpu.VMEM((128, 192), BF16),
            pltpu.VMEM((256, 256), BF16),
            pltpu.VMEM((2, 2, 5, 8, 128), F32),
            pltpu.VMEM((2, 8, 128), F32),
            pltpu.VMEM((2, 2, 5, 8, 128), F32),
            pltpu.VMEM((2, 2, 5, 8, 128), F32),
            pltpu.VMEM((2, 2, 8, 128), F32),
            pltpu.VMEM((4 * blocks, 128), F32),
            pltpu.VMEM((3 * blocks, 8 * group), BF16),
            pltpu.VMEM((group, 8, 128), F32),
            pltpu.VMEM((group, 8, 128), F32),
            pltpu.VMEM((group, 128, 256), BF16),
            pltpu.VMEM((group, 64, 256), F32),
            pltpu.VMEM((group, 8, 128), F32),
            pltpu.VMEM((group, 8, 128), F32),
            pltpu.VMEM((3 * blocks, 128), F32),
            pltpu.SemaphoreType.DMA((len(arrays),)),
            pltpu.SemaphoreType.DMA((2, 6)),
            pltpu.SemaphoreType.DMA((2, 6)),
            pltpu.SemaphoreType.DMA((2,)),
            pltpu.SemaphoreType.DMA((2, 8)),
        ],
        compiler_params=pltpu.CompilerParams(
            collective_id=0, has_side_effects=True, vmem_limit_bytes=40 * 1024 * 1024
        ),
    )(*[pltpu.with_memory_space_constraint(array, pltpu.HBM) for array in arrays])


def solution(mesh):
    sizes = tuple(mesh.shape[axis] for axis in ("gx", "gy", "gz"))
    return jax.shard_map(
        functools.partial(shards, sizes),
        mesh=mesh,
        in_specs=(
            P(None, "gx", "gy", "gz"),
            P(None, ("gx", "gy", "gz")),
            P(("gx", "gy", "gz")),
            P(("gx", "gy", "gz"), None),
        ),
        out_specs=(P(None, "gx", "gy", "gz"), P(None, ("gx", "gy", "gz"))),
        check_vma=False,
    )
```

```python
import functools

import jax
import jax.numpy as jnp
import numpy as np
from jax import lax
from jax.experimental import pallas as pl
from jax.experimental.pallas import tpu as pltpu
from jax.sharding import PartitionSpec as P

TIME_STEP = 0.01
LIFT = 14.0
ADVANCE = 0.5
F32 = jnp.float32
BF16 = jnp.bfloat16
MESH = pl.DeviceIdType.MESH


def gll_nodes():
    return np.array(
        [
            -1.0,
            -0.8717401485096066,
            -0.5917001814331423,
            -0.2092992179024789,
            0.2092992179024789,
            0.5917001814331423,
            0.8717401485096066,
            1.0,
        ]
    )


def legendre_seven(value):
    lower = 1.0
    upper = value
    for order in range(1, 7):
        lower, upper = (upper, ((2 * order + 1) * value * upper - order * lower) / (order + 1))
    return upper


def derivative_matrix():
    points = gll_nodes()
    legendre_at = [legendre_seven(float(points[i])) for i in range(8)]
    matrix = np.zeros((8, 8))
    for i in range(8):
        for m in range(8):
            if i != m:
                matrix[i, m] = legendre_at[i] / (legendre_at[m] * (points[i] - points[m]))
    matrix[0, 0] = -14.0
    matrix[7, 7] = 14.0
    return matrix


def constants():
    element = -derivative_matrix()
    element[0, 0] -= LIFT
    element[7, 7] += LIFT
    element = element * TIME_STEP
    eye = np.eye(8)
    planes = np.concatenate([np.kron(element, eye), np.kron(eye, element)], 0)
    line = np.kron(np.eye(16), element)
    for e in range(1, 16):
        line[8 * e, 8 * e - 1] = LIFT * TIME_STEP
        line[8 * e - 1, 8 * e] = -LIFT * TIME_STEP
    line = line.T
    points = gll_nodes()
    rows = np.zeros((8, 8))
    for n in range(8):
        others = [points[m] for m in range(8) if m != n]
        rows[:7, n] = others
        rows[7, n] = 1.0 / np.prod([points[n] - other for other in others])
    nodes = np.broadcast_to(rows[:, :, None], (8, 8, 128)).astype(np.float32)
    return planes.astype(np.float32), line.astype(np.float32), nodes


def slab_offsets(rows, chips):
    def distance(offset):
        dy, dc, _ = offset
        return min(dy, rows - dy) + min(dc, chips - dc)

    offsets = sorted(
        [(dy, dc, cx) for dy in range(rows) for dc in range(chips) for cx in range(2)],
        key=lambda offset: (distance(offset),) + offset,
    )
    opposite = [offsets.index(((rows - dy) % rows, (chips - dc) % chips, cx)) for dy, dc, cx in offsets]
    rings = [
        [k for k, offset in enumerate(offsets) if distance(offset) == d]
        for d in range(distance(offsets[-1]) + 1)
    ]
    return offsets, opposite, rings


def halves(value):
    high = value.astype(BF16)
    low = (value - high.astype(F32)).astype(BF16)
    return high, low


def dot(a, b):
    return jnp.dot(a, b, preferred_element_type=F32)


def body(
    sizes,
    fields_hbm,
    tracer_hbm,
    host_hbm,
    owner_hbm,
    planes_hbm,
    line_hbm,
    nodes_hbm,
    final,
    returned,
    tracer,
    slots,
    state,
    half,
    part,
    host,
    owner,
    planes_f32,
    line_f32,
    nodes,
    planes,
    line,
    y_out,
    z_out,
    x_in,
    y_in,
    z_in,
    payload,
    outgoing,
    received,
    z_weights,
    xy_weights,
    velocity,
    load_sem,
    halo_send,
    halo_recv,
    route_send,
    route_recv,
):
    n_gx, n_gy, n_gz, blocks = sizes
    group = n_gy * n_gz
    gx, gy, gz = lax.axis_index("gx"), lax.axis_index("gy"), lax.axis_index("gz")
    me = gy * n_gz + gz
    offsets, opposite, rings = slab_offsets(n_gy, n_gz // 2)

    loads = [
        pltpu.make_async_copy(source, target, load_sem.at[i])
        for i, (source, target) in enumerate(
            [
                (fields_hbm, state),
                (owner_hbm, owner),
                (tracer_hbm, tracer),
                (host_hbm, host),
                (planes_hbm, planes_f32),
                (line_hbm, line_f32),
                (nodes_hbm, nodes),
            ]
        )
    ]
    chip, core = lax.div(gz, 2), lax.rem(gz, 2)
    rows_to = [gy] + [lax.rem(gy + dy, n_gy) for dy in range(1, n_gy)]
    chips_to = [chip] + [lax.rem(chip + dc, n_gz // 2) for dc in range(1, n_gz // 2)]
    cores_to = [core, 1 - core]

    def peer(k):
        dy, dc, cx = offsets[k]
        return rows_to[dy], chips_to[dc] * 2 + cores_to[cx]

    has_low, has_high = gx > 0, gx < n_gx - 1
    x_low, x_high = jnp.maximum(gx - 1, 0), jnp.minimum(gx + 1, n_gx - 1)
    y_low, y_high = lax.rem(gy + n_gy - 1, n_gy), lax.rem(gy + 1, n_gy)
    z_low, z_high = lax.rem(gz + n_gz - 1, n_gz), lax.rem(gz + 1, n_gz)

    barrier = pltpu.get_barrier_semaphore()
    for k in range(group - 1, 0, -1):
        pl.semaphore_signal(barrier, inc=1, device_id=(gx,) + peer(k), device_id_type=MESH)
    for x, present in ((x_low, has_low), (x_high, has_high)):

        @pl.when(present)
        def _(x=x):
            pl.semaphore_signal(barrier, inc=1, device_id=(x, gy, gz), device_id_type=MESH)

    for i in (2, 1, 3, 0, 4, 5, 6):
        loads[i].start()

    for side, present in ((0, has_low), (1, has_high)):

        @pl.when(jnp.logical_not(present))
        def _(side=side):
            for step in range(2):
                x_in[step, side] = jnp.zeros_like(x_in[step, side])

    sends_when = [has_low, has_high, None, None, None, None]
    comes_when = [has_high, has_low, None, None, None, None]

    def each(copies, conditions, act):
        for copy, condition in zip(copies, conditions):
            if condition is None:
                act(copy)
            else:
                pl.when(condition)(functools.partial(act, copy))

    def start_halos(copies):
        each(copies, sends_when, lambda copy: copy.start())

    def await_halos(copies):
        each(copies, comes_when, lambda copy: copy.wait_recv())


    lane = lax.broadcasted_iota(jnp.int32, (8, 128), 1)
    sub = lax.broadcasted_iota(jnp.int32, (8, 128), 0)

    def fill_halos(source, step):
        for f in range(5):
            y_out[step, 0, f] = source[f, :, 0, :]
            y_out[step, 1, f] = source[f, :, 7, :]
        packed = jnp.zeros((8, 128), F32)
        for f in range(5):
            for x in range(8):
                at = f * 8 + x
                packed = jnp.where(
                    lane // 2 == at, pltpu.roll(source[f, x], (1 + 2 * at) % 128, 1), packed
                )
        z_out[step] = packed

    def halo_copies(source, step):
        sides = [
            (source.at[:, 0], x_in.at[step, 1], (x_low, gy, gz)),
            (source.at[:, 7], x_in.at[step, 0], (x_high, gy, gz)),
            (y_out.at[step, 0], y_in.at[step, 1], (gx, y_low, gz)),
            (y_out.at[step, 1], y_in.at[step, 0], (gx, y_high, gz)),
            (z_out.at[step], z_in.at[step, 1], (gx, gy, z_low)),
            (z_out.at[step], z_in.at[step, 0], (gx, gy, z_high)),
        ]
        return [
            pltpu.make_async_remote_copy(
                src_ref=source_ref,
                dst_ref=target_ref,
                send_sem=halo_send.at[step, i],
                recv_sem=halo_recv.at[step, i],
                device_id=device,
                device_id_type=MESH,
            )
            for i, (source_ref, target_ref, device) in enumerate(sides)
        ]

    def inner(source):
        wind = [source[d].reshape(64, 128) for d in range(3)]
        for f in range(5):
            value = source[f].reshape(64, 128)
            high, low = halves(value)
            across = dot(planes[...], jnp.concatenate([high, low, high], 0))
            along = dot(jnp.concatenate([high, low], 1), line[...])
            total = value + wind[0] * across[:64] + wind[1] * across[64:]
            total = total + wind[2] * (along[:, :128] + along[:, 128:])
            part[f] = total.reshape(8, 8, 128)

    lift = LIFT * TIME_STEP
    x_prev = jnp.where(gx == 0, 0.0, lift)
    x_next = jnp.where(gx == n_gx - 1, 0.0, -lift)
    y_prev = jnp.where(sub == 0, jnp.where(gy == 0, 0.0, lift), 0.0)
    y_next = jnp.where(sub == 7, jnp.where(gy == n_gy - 1, 0.0, -lift), 0.0)
    z_side = jnp.where(lane == 0, lift, 0.0) + jnp.where(lane == 127, -lift, 0.0)

    def outer(source, target, step):
        merged = jnp.where(
            lane % 2 == 0,
            pltpu.roll(z_in[step, 1], 127, 1),
            pltpu.roll(z_in[step, 0], 1, 1),
        )
        for x in range(8):
            wind = [source[d, x] for d in range(3)]
            y_wind = (wind[1] * y_prev, wind[1] * y_next)
            z_wind = wind[2] * z_side
            for f in range(5):
                at = f * 8 + x
                total = part[f, x]
                if x == 0:
                    total = total + wind[0] * (x_prev * x_in[step, 0, f])
                if x == 7:
                    total = total + wind[0] * (x_next * x_in[step, 1, f])
                total = total + y_wind[0] * y_in[step, 0, f, pl.ds(x, 1), :]
                total = total + y_wind[1] * y_in[step, 1, f, pl.ds(x, 1), :]
                total = total + z_wind * pltpu.roll(merged, (127 - 2 * at) % 128, 1)
                target[f, x] = total

    for load in loads[1:4]:
        load.wait()
    square = jnp.broadcast_to(owner[...].astype(F32), (blocks, blocks))
    diagonal = lax.broadcasted_iota(jnp.int32, (blocks, blocks), 0) == lax.broadcasted_iota(
        jnp.int32, (blocks, blocks), 1
    )
    owner_column = jnp.sum(jnp.where(diagonal, square, 0.0), axis=1, keepdims=True)
    owner_column = jnp.broadcast_to(owner_column, (blocks, 128))
    row = lax.broadcasted_iota(jnp.int32, (blocks, 128), 0)
    column = lax.broadcasted_iota(jnp.int32, (blocks, 128), 1)
    block_lane = lax.rem(column, blocks)
    owner_lane = jnp.sum(jnp.where(row == block_lane, owner_column, 0.0), axis=0, keepdims=True)
    same = owner_column == owner_lane
    earlier_lane = jnp.sum(
        jnp.where(same & (row < block_lane), 1.0, 0.0), axis=0, keepdims=True
    )
    earlier_column = jnp.sum(
        jnp.where(same & (column < row), 1.0, 0.0), axis=1, keepdims=True
    )
    slot_lane = owner_lane * 8.0 + earlier_lane * 4.0
    slot_column = owner_column[:, :1] * 8.0 + earlier_column * 4.0
    slots[...] = jnp.broadcast_to(slot_column, (blocks, 128))
    for b in range(blocks):
        payload[pl.ds(b, 3, stride=blocks), :] = tracer[:, b * 128 : (b + 1) * 128]
    payload[3 * blocks :, :] = host[...].astype(F32)
    width = 4 * blocks
    tall = lax.broadcasted_iota(jnp.int32, (group * 8, width), 0).astype(F32)
    part_lane = lax.broadcasted_iota(jnp.int32, (1, width), 1) // blocks
    target_row = slot_lane[:, :width] + part_lane.astype(F32)
    place = jnp.where(tall == target_row, 1.0, 0.0).astype(BF16)
    high, low = halves(payload[...])
    packed = dot(
        jnp.concatenate([place, place], 1), jnp.concatenate([high, low], 0)
    )
    outgoing[...] = packed.reshape(group, 8, 128)

    loads[4].wait()
    loads[5].wait()
    high, low = halves(planes_f32[...])
    planes[...] = jnp.concatenate([high, high, low], 1)
    high, low = halves(line_f32[...])
    line[:128, :128] = high
    line[128:, :128] = high
    line[:128, 128:] = low
    line[128:, 128:] = jnp.zeros_like(low)

    loads[0].wait()
    fill_halos(state, 0)

    pl.semaphore_wait(barrier, group - 1 + has_low.astype(jnp.int32) + has_high.astype(jnp.int32))

    def send_block(k):
        to_y, to_z = peer(k)
        pltpu.make_async_remote_copy(
            src_ref=outgoing.at[to_y * n_gz + to_z],
            dst_ref=received.at[opposite[k]],
            send_sem=route_send.at[0],
            recv_sem=route_recv.at[0, ring_of(k)],
            device_id=(gx, to_y, to_z),
            device_id_type=MESH,
        ).start()

    def ring_of(k):
        return [i for i, ring in enumerate(rings) if k in ring][0]

    far = [k for ring in rings[3:][::-1] for k in ring]
    near = [k for ring in rings[:3][::-1] for k in ring if k > 0]
    for k in far:
        send_block(k)
    first = halo_copies(state, 0)
    start_halos(first)
    for k in near:
        send_block(k)
    received[0] = outgoing[me]

    inner(state)
    await_halos(first)
    outer(state, half, 0)
    fill_halos(half, 1)
    second = halo_copies(half, 1)
    start_halos(second)

    loads[6].wait()
    table = half[0:3].reshape(192, 128).astype(BF16)
    lower_half = jnp.where(lax.broadcasted_iota(jnp.int32, (16, 128), 0) >= 8, 1.0, 0.0)

    def lagrange(coordinate):
        value = nodes[7]
        for k in range(7):
            value = value * (coordinate - nodes[k])
        return value

    def weigh(s):
        for a in range(2):
            lanes = slice(a * 128, (a + 1) * 128)
            coordinate = [received[s, 4 * a + c : 4 * a + c + 1, :] for c in range(4)]
            along = [lagrange(coordinate[c]) for c in range(3)]
            pair = jnp.concatenate([along[2], along[2]], 0).astype(BF16)
            even = (coordinate[3] - lower_half).astype(BF16)
            for e in range(8):
                z_weights[s, e * 16 : (e + 1) * 16, lanes] = jnp.where(
                    even == jnp.asarray(2 * e, BF16), pair, jnp.zeros_like(pair)
                )
            xy_weights[s, 0:8, lanes] = along[0]
            xy_weights[s, 8:16, lanes] = along[1]

    def interpolate(s):
        values = dot(table, z_weights[s])
        for a in range(2):
            lanes = slice(a * 128, (a + 1) * 128)
            rows = []
            for c in range(3):
                total = xy_weights[s, 0:1, lanes] * values[c * 64 : c * 64 + 8, lanes]
                for i in range(1, 8):
                    at = c * 64 + i * 8
                    total = total + xy_weights[s, i : i + 1, lanes] * values[at : at + 8, lanes]
                rows.append(
                    jnp.sum(total * xy_weights[s, 8:16, lanes], axis=0, keepdims=True)
                )
            velocity[s, 4 * a : 4 * a + 4, :] = jnp.concatenate(rows + [jnp.zeros_like(rows[0])], 0)

    def ring_bytes(ring, buffer):
        return buffer.at[pl.ds(0, len([k for k in ring if k > 0]))]

    def weigh_ring(i):
        ring = rings[i]
        span = ring_bytes(ring, received)
        pltpu.make_async_copy(span, span, route_recv.at[0, i]).wait()

        def step(s, carry):
            weigh(s)
            return carry

        lax.fori_loop(ring[0], ring[-1] + 1, step, 0)

    def answer_ring(i):
        for k in rings[i]:
            interpolate(k)
        for k in rings[i]:
            if k == 0:
                returned[me] = velocity[0]
                continue
            pltpu.make_async_remote_copy(
                src_ref=velocity.at[k],
                dst_ref=returned.at[me],
                send_sem=route_send.at[1],
                recv_sem=route_recv.at[1, 0],
                device_id=(gx,) + peer(k),
                device_id_type=MESH,
            ).start()

    last = len(rings) - 1
    for i in [0, 1]:
        weigh_ring(i)
    for i in range(last, 1, -1):
        weigh_ring(i)
        answer_ring(i)
    for i in [1, 0]:
        answer_ring(i)

    inner(half)
    await_halos(second)
    outer(half, final, 1)

    others = returned.at[pl.ds(0, group - 1)]
    pltpu.make_async_copy(others, others, route_recv.at[1, 0]).wait()
    for copies in (first, second):
        each(copies, sends_when, lambda copy: copy.wait_send())
    others = outgoing.at[pl.ds(0, group - 1)]
    pltpu.make_async_copy(others, others, route_send.at[0]).wait()
    others = velocity.at[pl.ds(0, group - 1)]
    pltpu.make_async_copy(others, others, route_send.at[1]).wait()


def finish(final, returned, tracer, slots, final_hbm, moved_hbm, own_velocity, moved, store_sem):
    store = pltpu.make_async_copy(final, final_hbm, store_sem.at[0])
    store.start()
    blocks, group = slots.shape[0], returned.shape[0]
    high, low = halves(returned[...].reshape(group * 8, 128))
    wide = lax.broadcasted_iota(jnp.int32, (blocks, group * 8), 1).astype(F32)
    unpack = jnp.concatenate(
        [jnp.where(wide == slots[:, :1] + float(c), 1.0, 0.0).astype(BF16) for c in range(3)], 0
    )
    own_velocity[...] = dot(unpack, high) + dot(unpack, low)
    for b in range(blocks):
        lanes = slice(b * 128, (b + 1) * 128)
        moved[:, lanes] = (
            tracer[:, lanes] + ADVANCE * own_velocity[pl.ds(b, 3, stride=blocks), :]
        )
    store_moved = pltpu.make_async_copy(moved, moved_hbm, store_sem.at[1])
    store_moved.start()
    store.wait()
    store_moved.wait()


def shards(sizes, fields, tracer_ref, host_element, block_owner):
    n_gx, n_gy, n_gz = sizes
    group = n_gy * n_gz
    blocks = block_owner.shape[0]
    planes, line, nodes = constants()
    arrays = (
        fields,
        tracer_ref,
        host_element.reshape(blocks, 128),
        block_owner.reshape(1, blocks),
        jnp.asarray(planes),
        jnp.asarray(line),
        jnp.asarray(nodes),
    )
    in_hbm = pl.BlockSpec(memory_space=pltpu.HBM)
    in_vmem = pl.BlockSpec(memory_space=pltpu.VMEM)
    results = pl.pallas_call(
        functools.partial(body, (n_gx, n_gy, n_gz, blocks)),
        out_shape=(
            jax.ShapeDtypeStruct(fields.shape, F32),
            jax.ShapeDtypeStruct((group, 8, 128), F32),
            jax.ShapeDtypeStruct(tracer_ref.shape, F32),
            jax.ShapeDtypeStruct((blocks, 128), F32),
        ),
        in_specs=[in_hbm] * len(arrays),
        out_specs=(in_vmem,) * 4,
        scratch_shapes=[
            pltpu.VMEM(fields.shape, F32),
            pltpu.VMEM(fields.shape, F32),
            pltpu.VMEM(fields.shape, F32),
            pltpu.VMEM((blocks, 128), jnp.int32),
            pltpu.VMEM((1, blocks), jnp.int32),
            pltpu.VMEM(planes.shape, F32),
            pltpu.VMEM(line.shape, F32),
            pltpu.VMEM(nodes.shape, F32),
            pltpu.VMEM((128, 192), BF16),
            pltpu.VMEM((256, 256), BF16),
            pltpu.VMEM((2, 2, 5, 8, 128), F32),
            pltpu.VMEM((2, 8, 128), F32),
            pltpu.VMEM((2, 2, 5, 8, 128), F32),
            pltpu.VMEM((2, 2, 5, 8, 128), F32),
            pltpu.VMEM((2, 2, 8, 128), F32),
            pltpu.VMEM((4 * blocks, 128), F32),
            pltpu.VMEM((group, 8, 128), F32),
            pltpu.VMEM((group, 8, 128), F32),
            pltpu.VMEM((group, 128, 256), BF16),
            pltpu.VMEM((group, 16, 256), F32),
            pltpu.VMEM((group, 8, 128), F32),
            pltpu.SemaphoreType.DMA((len(arrays),)),
            pltpu.SemaphoreType.DMA((2, 6)),
            pltpu.SemaphoreType.DMA((2, 6)),
            pltpu.SemaphoreType.DMA((2,)),
            pltpu.SemaphoreType.DMA((2, 8)),
        ],
        compiler_params=pltpu.CompilerParams(
            collective_id=0, has_side_effects=True, vmem_limit_bytes=40 * 1024 * 1024
        ),
    )(*[pltpu.with_memory_space_constraint(array, pltpu.HBM) for array in arrays])
    return pl.pallas_call(
        finish,
        out_shape=(
            jax.ShapeDtypeStruct(fields.shape, F32),
            jax.ShapeDtypeStruct(tracer_ref.shape, F32),
        ),
        in_specs=[in_vmem] * 4,
        out_specs=(in_hbm, in_hbm),
        scratch_shapes=[
            pltpu.VMEM((3 * blocks, 128), F32),
            pltpu.VMEM(tracer_ref.shape, F32),
            pltpu.SemaphoreType.DMA((2,)),
        ],
        compiler_params=pltpu.CompilerParams(vmem_limit_bytes=2 * 1024 * 1024),
    )(*results)


def solution(mesh):
    sizes = tuple(mesh.shape[axis] for axis in ("gx", "gy", "gz"))
    return jax.shard_map(
        functools.partial(shards, sizes),
        mesh=mesh,
        in_specs=(
            P(None, "gx", "gy", "gz"),
            P(None, ("gx", "gy", "gz")),
            P(("gx", "gy", "gz")),
            P(("gx", "gy", "gz"), None),
        ),
        out_specs=(P(None, "gx", "gy", "gz"), P(None, ("gx", "gy", "gz"))),
        check_vma=False,
    )
```

```python
import functools

import jax
import jax.numpy as jnp
import numpy as np
from jax import lax
from jax.experimental import pallas as pl
from jax.experimental.pallas import tpu as pltpu
from jax.sharding import PartitionSpec as P

TIME_STEP = 0.01
LIFT = 14.0
ADVANCE = 0.5
F32 = jnp.float32
BF16 = jnp.bfloat16
MESH = pl.DeviceIdType.MESH


def gll_nodes():
    return np.array(
        [
            -1.0,
            -0.8717401485096066,
            -0.5917001814331423,
            -0.2092992179024789,
            0.2092992179024789,
            0.5917001814331423,
            0.8717401485096066,
            1.0,
        ]
    )


def legendre_seven(value):
    lower = 1.0
    upper = value
    for order in range(1, 7):
        lower, upper = (upper, ((2 * order + 1) * value * upper - order * lower) / (order + 1))
    return upper


def derivative_matrix():
    points = gll_nodes()
    legendre_at = [legendre_seven(float(points[i])) for i in range(8)]
    matrix = np.zeros((8, 8))
    for i in range(8):
        for m in range(8):
            if i != m:
                matrix[i, m] = legendre_at[i] / (legendre_at[m] * (points[i] - points[m]))
    matrix[0, 0] = -14.0
    matrix[7, 7] = 14.0
    return matrix


def constants():
    element = -derivative_matrix()
    element[0, 0] -= LIFT
    element[7, 7] += LIFT
    element = element * TIME_STEP
    eye = np.eye(8)
    planes = np.concatenate([np.kron(element, eye), np.kron(eye, element)], 0)
    line = np.kron(np.eye(16), element)
    for e in range(1, 16):
        line[8 * e, 8 * e - 1] = LIFT * TIME_STEP
        line[8 * e - 1, 8 * e] = -LIFT * TIME_STEP
    line = line.T
    points = gll_nodes()
    rows = np.zeros((8, 8))
    for n in range(8):
        others = [points[m] for m in range(8) if m != n]
        rows[:7, n] = others
        rows[7, n] = 1.0 / np.prod([points[n] - other for other in others])
    nodes = np.broadcast_to(rows[:, :, None], (8, 8, 128)).astype(np.float32)
    return planes.astype(np.float32), line.astype(np.float32), nodes


def slab_offsets(rows, chips):
    def distance(offset):
        dy, dc = offset
        return min(dy, rows - dy) + min(dc, chips - dc)

    offsets = sorted(
        [(dy, dc) for dy in range(rows) for dc in range(chips)],
        key=lambda offset: (distance(offset),) + offset,
    )
    opposite = [offsets.index(((rows - dy) % rows, (chips - dc) % chips)) for dy, dc in offsets]
    rings = [
        [k for k, offset in enumerate(offsets) if distance(offset) == d]
        for d in range(distance(offsets[-1]) + 1)
    ]
    return offsets, opposite, rings


def halves(value):
    high = value.astype(BF16)
    low = (value - high.astype(F32)).astype(BF16)
    return high, low


def dot(a, b):
    return jnp.dot(a, b, preferred_element_type=F32)


def body(
    sizes,
    fields_hbm,
    tracer_hbm,
    host_hbm,
    owner_hbm,
    planes_hbm,
    line_hbm,
    nodes_hbm,
    final,
    returned,
    tracer,
    slots,
    state,
    half,
    part,
    host,
    owner,
    planes_f32,
    line_f32,
    nodes,
    planes,
    line,
    y_out,
    z_out,
    x_in,
    y_in,
    z_in,
    payload,
    outgoing,
    received,
    z_weights,
    xy_weights,
    velocity,
    sibling,
    tables,
    load_sem,
    halo_send,
    halo_recv,
    route_send,
    route_recv,
    table_sem,
):
    n_gx, n_gy, n_gz, blocks = sizes
    group, chips = n_gy * n_gz, n_gy * (n_gz // 2)
    gx, gy, gz = lax.axis_index("gx"), lax.axis_index("gy"), lax.axis_index("gz")
    offsets, opposite, rings = slab_offsets(n_gy, n_gz // 2)

    loads = [
        pltpu.make_async_copy(source, target, load_sem.at[i])
        for i, (source, target) in enumerate(
            [
                (fields_hbm, state),
                (owner_hbm, owner),
                (tracer_hbm, tracer),
                (host_hbm, host),
                (planes_hbm, planes_f32),
                (line_hbm, line_f32),
                (nodes_hbm, nodes),
            ]
        )
    ]
    chip, core = lax.div(gz, 2), lax.rem(gz, 2)
    rows_to = [gy] + [lax.rem(gy + dy, n_gy) for dy in range(1, n_gy)]
    chips_to = [chip] + [lax.rem(chip + dc, n_gz // 2) for dc in range(1, n_gz // 2)]
    me = gy * (n_gz // 2) + chip

    def peer(k):
        dy, dc = offsets[k]
        return rows_to[dy], chips_to[dc] * 2 + core

    has_low, has_high = gx > 0, gx < n_gx - 1
    x_low, x_high = jnp.maximum(gx - 1, 0), jnp.minimum(gx + 1, n_gx - 1)
    y_low, y_high = lax.rem(gy + n_gy - 1, n_gy), lax.rem(gy + 1, n_gy)
    z_low, z_high = lax.rem(gz + n_gz - 1, n_gz), lax.rem(gz + 1, n_gz)

    barrier = pltpu.get_barrier_semaphore()
    for k in range(chips - 1, 0, -1):
        pl.semaphore_signal(barrier, inc=1, device_id=(gx,) + peer(k), device_id_type=MESH)
    for z in (z_low, z_high):
        pl.semaphore_signal(barrier, inc=1, device_id=(gx, gy, z), device_id_type=MESH)
    for x, present in ((x_low, has_low), (x_high, has_high)):

        @pl.when(present)
        def _(x=x):
            pl.semaphore_signal(barrier, inc=1, device_id=(x, gy, gz), device_id_type=MESH)

    for i in (2, 1, 3, 0, 4, 5, 6):
        loads[i].start()

    for side, present in ((0, has_low), (1, has_high)):

        @pl.when(jnp.logical_not(present))
        def _(side=side):
            for step in range(2):
                x_in[step, side] = jnp.zeros_like(x_in[step, side])

    sends_when = [has_low, has_high, None, None, None, None]
    comes_when = [has_high, has_low, None, None, None, None]

    def each(copies, conditions, act):
        for copy, condition in zip(copies, conditions):
            if condition is None:
                act(copy)
            else:
                pl.when(condition)(functools.partial(act, copy))

    def start_halos(copies):
        each(copies, sends_when, lambda copy: copy.start())

    def await_halos(copies):
        each(copies, comes_when, lambda copy: copy.wait_recv())


    lane = lax.broadcasted_iota(jnp.int32, (8, 128), 1)
    sub = lax.broadcasted_iota(jnp.int32, (8, 128), 0)

    def fill_halos(source, step):
        for f in range(5):
            y_out[step, 0, f] = source[f, :, 0, :]
            y_out[step, 1, f] = source[f, :, 7, :]
        packed = jnp.zeros((8, 128), F32)
        for f in range(5):
            for x in range(8):
                at = f * 8 + x
                packed = jnp.where(
                    lane // 2 == at, pltpu.roll(source[f, x], (1 + 2 * at) % 128, 1), packed
                )
        z_out[step] = packed

    def halo_copies(source, step):
        sides = [
            (source.at[:, 0], x_in.at[step, 1], (x_low, gy, gz)),
            (source.at[:, 7], x_in.at[step, 0], (x_high, gy, gz)),
            (y_out.at[step, 0], y_in.at[step, 1], (gx, y_low, gz)),
            (y_out.at[step, 1], y_in.at[step, 0], (gx, y_high, gz)),
            (z_out.at[step], z_in.at[step, 1], (gx, gy, z_low)),
            (z_out.at[step], z_in.at[step, 0], (gx, gy, z_high)),
        ]
        return [
            pltpu.make_async_remote_copy(
                src_ref=source_ref,
                dst_ref=target_ref,
                send_sem=halo_send.at[step, i],
                recv_sem=halo_recv.at[step, i],
                device_id=device,
                device_id_type=MESH,
            )
            for i, (source_ref, target_ref, device) in enumerate(sides)
        ]

    def inner(source):
        wind = [source[d].reshape(64, 128) for d in range(3)]
        for f in range(5):
            value = source[f].reshape(64, 128)
            high, low = halves(value)
            across = dot(planes[...], jnp.concatenate([high, low, high], 0))
            along = dot(jnp.concatenate([high, low], 1), line[...])
            total = value + wind[0] * across[:64] + wind[1] * across[64:]
            total = total + wind[2] * (along[:, :128] + along[:, 128:])
            part[f] = total.reshape(8, 8, 128)

    lift = LIFT * TIME_STEP
    x_prev = jnp.where(gx == 0, 0.0, lift)
    x_next = jnp.where(gx == n_gx - 1, 0.0, -lift)
    y_prev = jnp.where(sub == 0, jnp.where(gy == 0, 0.0, lift), 0.0)
    y_next = jnp.where(sub == 7, jnp.where(gy == n_gy - 1, 0.0, -lift), 0.0)
    z_side = jnp.where(lane == 0, lift, 0.0) + jnp.where(lane == 127, -lift, 0.0)

    def outer(source, target, step):
        merged = jnp.where(
            lane % 2 == 0,
            pltpu.roll(z_in[step, 1], 127, 1),
            pltpu.roll(z_in[step, 0], 1, 1),
        )
        for x in range(8):
            wind = [source[d, x] for d in range(3)]
            y_wind = (wind[1] * y_prev, wind[1] * y_next)
            z_wind = wind[2] * z_side
            for f in range(5):
                at = f * 8 + x
                total = part[f, x]
                if x == 0:
                    total = total + wind[0] * (x_prev * x_in[step, 0, f])
                if x == 7:
                    total = total + wind[0] * (x_next * x_in[step, 1, f])
                total = total + y_wind[0] * y_in[step, 0, f, pl.ds(x, 1), :]
                total = total + y_wind[1] * y_in[step, 1, f, pl.ds(x, 1), :]
                total = total + z_wind * pltpu.roll(merged, (127 - 2 * at) % 128, 1)
                target[f, x] = total

    for load in loads[1:4]:
        load.wait()
    square = jnp.broadcast_to(owner[...].astype(F32), (blocks, blocks))
    diagonal = lax.broadcasted_iota(jnp.int32, (blocks, blocks), 0) == lax.broadcasted_iota(
        jnp.int32, (blocks, blocks), 1
    )
    owner_column = jnp.sum(jnp.where(diagonal, square, 0.0), axis=1, keepdims=True)
    owner_column = jnp.broadcast_to(owner_column, (blocks, 128))
    row = lax.broadcasted_iota(jnp.int32, (blocks, 128), 0)
    column = lax.broadcasted_iota(jnp.int32, (blocks, 128), 1)
    block_lane = lax.rem(column, blocks)
    owner_lane = jnp.sum(jnp.where(row == block_lane, owner_column, 0.0), axis=0, keepdims=True)
    same = owner_column == owner_lane
    earlier_lane = jnp.sum(
        jnp.where(same & (row < block_lane), 1.0, 0.0), axis=0, keepdims=True
    )
    earlier_column = jnp.sum(
        jnp.where(same & (column < row), 1.0, 0.0), axis=1, keepdims=True
    )
    slot_lane = owner_lane * 8.0 + earlier_lane * 4.0
    slot_column = owner_column[:, :1] * 8.0 + earlier_column * 4.0
    slots[...] = jnp.broadcast_to(slot_column, (blocks, 128))
    for b in range(blocks):
        payload[pl.ds(b, 3, stride=blocks), :] = tracer[:, b * 128 : (b + 1) * 128]
    payload[3 * blocks :, :] = host[...].astype(F32)
    width = 4 * blocks
    tall = lax.broadcasted_iota(jnp.int32, (group * 8, width), 0).astype(F32)
    part_lane = lax.broadcasted_iota(jnp.int32, (1, width), 1) // blocks
    target_row = slot_lane[:, :width] + part_lane.astype(F32)
    place = jnp.where(tall == target_row, 1.0, 0.0).astype(BF16)
    high, low = halves(payload[...])
    packed = dot(
        jnp.concatenate([place, place], 1), jnp.concatenate([high, low], 0)
    )
    outgoing[...] = packed.reshape(chips, 2, 8, 128)

    loads[4].wait()
    loads[5].wait()
    high, low = halves(planes_f32[...])
    planes[...] = jnp.concatenate([high, high, low], 1)
    high, low = halves(line_f32[...])
    line[:128, :128] = high
    line[128:, :128] = high
    line[:128, 128:] = low
    line[128:, 128:] = jnp.zeros_like(low)

    loads[0].wait()
    fill_halos(state, 0)

    pl.semaphore_wait(barrier, chips + 1 + has_low.astype(jnp.int32) + has_high.astype(jnp.int32))

    def send_block(k):
        to_y, to_z = peer(k)
        pltpu.make_async_remote_copy(
            src_ref=outgoing.at[to_y * (n_gz // 2) + lax.div(to_z, 2)],
            dst_ref=received.at[opposite[k]],
            send_sem=route_send.at[0],
            recv_sem=route_recv.at[0, ring_of(k)],
            device_id=(gx, to_y, to_z),
            device_id_type=MESH,
        ).start()

    def ring_of(k):
        return [i for i, ring in enumerate(rings) if k in ring][0]

    far = [k for ring in rings[3:][::-1] for k in ring]
    near = [k for ring in rings[:3][::-1] for k in ring if k > 0]
    for k in far:
        send_block(k)
    first = halo_copies(state, 0)
    start_halos(first)
    for k in near:
        send_block(k)
    received[0] = outgoing[me]

    inner(state)
    await_halos(first)
    outer(state, half, 0)
    fill_halos(half, 1)
    partner = pltpu.make_async_remote_copy(
        src_ref=half.at[pl.ds(0, 3)],
        dst_ref=sibling,
        send_sem=table_sem.at[0],
        recv_sem=table_sem.at[1],
        device_id=(gx, gy, chip * 2 + 1 - core),
        device_id_type=MESH,
    )
    partner.start()
    second = halo_copies(half, 1)
    start_halos(second)

    loads[6].wait()
    tables[core] = half[0:3].reshape(192, 128).astype(BF16)
    lower_half = jnp.where(lax.broadcasted_iota(jnp.int32, (16, 128), 0) >= 8, 1.0, 0.0)

    def lagrange(coordinate):
        value = nodes[7]
        for k in range(7):
            value = value * (coordinate - nodes[k])
        return value

    def weigh(k, owner):
        s = 2 * k + owner
        for a in range(2):
            lanes = slice(a * 128, (a + 1) * 128)
            coordinate = [
                received[k, owner, 4 * a + c : 4 * a + c + 1, :] for c in range(4)
            ]
            along = [lagrange(coordinate[c]) for c in range(3)]
            pair = jnp.concatenate([along[2], along[2]], 0).astype(BF16)
            even = (coordinate[3] - lower_half).astype(BF16)
            for e in range(8):
                z_weights[s, e * 16 : (e + 1) * 16, lanes] = jnp.where(
                    even == jnp.asarray(2 * e, BF16), pair, jnp.zeros_like(pair)
                )
            xy_weights[s, 0:8, lanes] = along[0]
            xy_weights[s, 8:16, lanes] = along[1]

    def interpolate(k, owner):
        s = 2 * k + owner
        values = dot(tables[owner], z_weights[s])
        for a in range(2):
            lanes = slice(a * 128, (a + 1) * 128)
            rows = []
            for c in range(3):
                total = xy_weights[s, 0:1, lanes] * values[c * 64 : c * 64 + 8, lanes]
                for i in range(1, 8):
                    at = c * 64 + i * 8
                    total = total + xy_weights[s, i : i + 1, lanes] * values[at : at + 8, lanes]
                rows.append(
                    jnp.sum(total * xy_weights[s, 8:16, lanes], axis=0, keepdims=True)
                )
            velocity[k, owner, 4 * a : 4 * a + 4, :] = jnp.concatenate(rows + [jnp.zeros_like(rows[0])], 0)

    def weigh_ring(i):
        ring = rings[i]
        if i > 0:
            span = received.at[pl.ds(0, len(ring))]
            pltpu.make_async_copy(span, span, route_recv.at[0, i]).wait()

        def step(k, carry):
            weigh(k, 0)
            weigh(k, 1)
            return carry

        lax.fori_loop(ring[0], ring[-1] + 1, step, 0)

    def answer_ring(i):
        for k in rings[i]:
            interpolate(k, 0)
            interpolate(k, 1)
        for k in rings[i]:
            if k == 0:
                returned[me] = velocity[0]
                continue
            pltpu.make_async_remote_copy(
                src_ref=velocity.at[k],
                dst_ref=returned.at[me],
                send_sem=route_send.at[1],
                recv_sem=route_recv.at[1, 0],
                device_id=(gx,) + peer(k),
                device_id_type=MESH,
            ).start()

    last = len(rings) - 1
    for i in [0, 1]:
        weigh_ring(i)
    partner.wait_recv()
    tables[1 - core] = sibling[...].reshape(192, 128).astype(BF16)
    for i in range(last, 1, -1):
        weigh_ring(i)
        answer_ring(i)
    for i in [1, 0]:
        answer_ring(i)

    inner(half)
    await_halos(second)
    outer(half, final, 1)

    others = returned.at[pl.ds(0, chips - 1)]
    pltpu.make_async_copy(others, others, route_recv.at[1, 0]).wait()
    partner.wait_send()
    for copies in (first, second):
        each(copies, sends_when, lambda copy: copy.wait_send())
    others = outgoing.at[pl.ds(0, chips - 1)]
    pltpu.make_async_copy(others, others, route_send.at[0]).wait()
    others = velocity.at[pl.ds(0, chips - 1)]
    pltpu.make_async_copy(others, others, route_send.at[1]).wait()


def finish(final, returned, tracer, slots, final_hbm, moved_hbm, own_velocity, moved, store_sem):
    store = pltpu.make_async_copy(final, final_hbm, store_sem.at[0])
    store.start()
    blocks, group = slots.shape[0], 2 * returned.shape[0]
    high, low = halves(returned[...].reshape(group * 8, 128))
    wide = lax.broadcasted_iota(jnp.int32, (blocks, group * 8), 1).astype(F32)
    unpack = jnp.concatenate(
        [jnp.where(wide == slots[:, :1] + float(c), 1.0, 0.0).astype(BF16) for c in range(3)], 0
    )
    own_velocity[...] = dot(unpack, high) + dot(unpack, low)
    for b in range(blocks):
        lanes = slice(b * 128, (b + 1) * 128)
        moved[:, lanes] = (
            tracer[:, lanes] + ADVANCE * own_velocity[pl.ds(b, 3, stride=blocks), :]
        )
    store_moved = pltpu.make_async_copy(moved, moved_hbm, store_sem.at[1])
    store_moved.start()
    store.wait()
    store_moved.wait()


def shards(sizes, fields, tracer_ref, host_element, block_owner):
    n_gx, n_gy, n_gz = sizes
    group, chips = n_gy * n_gz, n_gy * (n_gz // 2)
    blocks = block_owner.shape[0]
    planes, line, nodes = constants()
    arrays = (
        fields,
        tracer_ref,
        host_element.reshape(blocks, 128),
        block_owner.reshape(1, blocks),
        jnp.asarray(planes),
        jnp.asarray(line),
        jnp.asarray(nodes),
    )
    in_hbm = pl.BlockSpec(memory_space=pltpu.HBM)
    in_vmem = pl.BlockSpec(memory_space=pltpu.VMEM)
    results = pl.pallas_call(
        functools.partial(body, (n_gx, n_gy, n_gz, blocks)),
        out_shape=(
            jax.ShapeDtypeStruct(fields.shape, F32),
            jax.ShapeDtypeStruct((chips, 2, 8, 128), F32),
            jax.ShapeDtypeStruct(tracer_ref.shape, F32),
            jax.ShapeDtypeStruct((blocks, 128), F32),
        ),
        in_specs=[in_hbm] * len(arrays),
        out_specs=(in_vmem,) * 4,
        scratch_shapes=[
            pltpu.VMEM(fields.shape, F32),
            pltpu.VMEM(fields.shape, F32),
            pltpu.VMEM(fields.shape, F32),
            pltpu.VMEM((blocks, 128), jnp.int32),
            pltpu.VMEM((1, blocks), jnp.int32),
            pltpu.VMEM(planes.shape, F32),
            pltpu.VMEM(line.shape, F32),
            pltpu.VMEM(nodes.shape, F32),
            pltpu.VMEM((128, 192), BF16),
            pltpu.VMEM((256, 256), BF16),
            pltpu.VMEM((2, 2, 5, 8, 128), F32),
            pltpu.VMEM((2, 8, 128), F32),
            pltpu.VMEM((2, 2, 5, 8, 128), F32),
            pltpu.VMEM((2, 2, 5, 8, 128), F32),
            pltpu.VMEM((2, 2, 8, 128), F32),
            pltpu.VMEM((4 * blocks, 128), F32),
            pltpu.VMEM((chips, 2, 8, 128), F32),
            pltpu.VMEM((chips, 2, 8, 128), F32),
            pltpu.VMEM((group, 128, 256), BF16),
            pltpu.VMEM((group, 16, 256), F32),
            pltpu.VMEM((chips, 2, 8, 128), F32),
            pltpu.VMEM((3, 8, 8, 128), F32),
            pltpu.VMEM((2, 192, 128), BF16),
            pltpu.SemaphoreType.DMA((len(arrays),)),
            pltpu.SemaphoreType.DMA((2, 6)),
            pltpu.SemaphoreType.DMA((2, 6)),
            pltpu.SemaphoreType.DMA((2,)),
            pltpu.SemaphoreType.DMA((2, 8)),
            pltpu.SemaphoreType.DMA((2,)),
        ],
        compiler_params=pltpu.CompilerParams(
            collective_id=0, has_side_effects=True, vmem_limit_bytes=40 * 1024 * 1024
        ),
    )(*[pltpu.with_memory_space_constraint(array, pltpu.HBM) for array in arrays])
    return pl.pallas_call(
        finish,
        out_shape=(
            jax.ShapeDtypeStruct(fields.shape, F32),
            jax.ShapeDtypeStruct(tracer_ref.shape, F32),
        ),
        in_specs=[in_vmem] * 4,
        out_specs=(in_hbm, in_hbm),
        scratch_shapes=[
            pltpu.VMEM((3 * blocks, 128), F32),
            pltpu.VMEM(tracer_ref.shape, F32),
            pltpu.SemaphoreType.DMA((2,)),
        ],
        compiler_params=pltpu.CompilerParams(vmem_limit_bytes=2 * 1024 * 1024),
    )(*results)


def solution(mesh):
    sizes = tuple(mesh.shape[axis] for axis in ("gx", "gy", "gz"))
    return jax.shard_map(
        functools.partial(shards, sizes),
        mesh=mesh,
        in_specs=(
            P(None, "gx", "gy", "gz"),
            P(None, ("gx", "gy", "gz")),
            P(("gx", "gy", "gz")),
            P(("gx", "gy", "gz"), None),
        ),
        out_specs=(P(None, "gx", "gy", "gz"), P(None, ("gx", "gy", "gz"))),
        check_vma=False,
    )
```

```python
import functools

import jax
import jax.numpy as jnp
import numpy as np
from jax import lax
from jax.experimental import pallas as pl
from jax.experimental.pallas import tpu as pltpu
from jax.sharding import PartitionSpec as P

TIME_STEP = 0.01
LIFT = 14.0
ADVANCE = 0.5
F32 = jnp.float32
BF16 = jnp.bfloat16
MESH = pl.DeviceIdType.MESH


def gll_nodes():
    return np.array(
        [
            -1.0,
            -0.8717401485096066,
            -0.5917001814331423,
            -0.2092992179024789,
            0.2092992179024789,
            0.5917001814331423,
            0.8717401485096066,
            1.0,
        ]
    )


def legendre_seven(value):
    lower = 1.0
    upper = value
    for order in range(1, 7):
        lower, upper = (upper, ((2 * order + 1) * value * upper - order * lower) / (order + 1))
    return upper


def derivative_matrix():
    points = gll_nodes()
    legendre_at = [legendre_seven(float(points[i])) for i in range(8)]
    matrix = np.zeros((8, 8))
    for i in range(8):
        for m in range(8):
            if i != m:
                matrix[i, m] = legendre_at[i] / (legendre_at[m] * (points[i] - points[m]))
    matrix[0, 0] = -14.0
    matrix[7, 7] = 14.0
    return matrix


def constants():
    element = -derivative_matrix()
    element[0, 0] -= LIFT
    element[7, 7] += LIFT
    element = element * TIME_STEP
    eye = np.eye(8)
    planes = np.concatenate([np.kron(element, eye), np.kron(eye, element)], 0)
    line = np.kron(np.eye(16), element)
    for e in range(1, 16):
        line[8 * e, 8 * e - 1] = LIFT * TIME_STEP
        line[8 * e - 1, 8 * e] = -LIFT * TIME_STEP
    line = line.T
    return planes.astype(np.float32), line.astype(np.float32)


def slab_offsets(rows, chips):
    def distance(offset):
        dy, dc = offset
        return min(dy, rows - dy) + min(dc, chips - dc)

    every = [(dy, dc) for dy in range(rows) for dc in range(chips)]
    farthest = max(distance(offset) for offset in every)
    offsets = sorted(
        every,
        key=lambda offset: (0.5 if distance(offset) == farthest else distance(offset),) + offset,
    )
    opposite = [offsets.index(((rows - dy) % rows, (chips - dc) % chips)) for dy, dc in offsets]
    rings = [
        [k for k, offset in enumerate(offsets) if distance(offset) == d]
        for d in range(farthest + 1)
    ]
    return offsets, opposite, rings


def halves(value):
    high = value.astype(BF16)
    low = (value - high.astype(F32)).astype(BF16)
    return high, low


def dot(a, b):
    return jnp.dot(a, b, preferred_element_type=F32)


def body(
    sizes,
    fields_hbm,
    tracer_hbm,
    host_hbm,
    owner_hbm,
    planes_hbm,
    line_hbm,
    final,
    returned,
    tracer,
    slots,
    state,
    half,
    part,
    host,
    owner,
    planes_f32,
    line_f32,
    planes,
    line,
    y_out,
    z_out,
    x_in,
    y_in,
    z_in,
    payload,
    outgoing,
    received,
    z_weights,
    factors,
    velocity,
    sibling,
    tables,
    load_sem,
    halo_send,
    halo_recv,
    route_send,
    route_recv,
    table_sem,
):
    n_gx, n_gy, n_gz, blocks = sizes
    group, chips = n_gy * n_gz, n_gy * (n_gz // 2)
    gx, gy, gz = lax.axis_index("gx"), lax.axis_index("gy"), lax.axis_index("gz")
    offsets, opposite, rings = slab_offsets(n_gy, n_gz // 2)

    loads = [
        pltpu.make_async_copy(source, target, load_sem.at[i])
        for i, (source, target) in enumerate(
            [
                (fields_hbm, state),
                (owner_hbm, owner),
                (tracer_hbm, tracer),
                (host_hbm, host),
                (planes_hbm, planes_f32),
                (line_hbm, line_f32),
            ]
        )
    ]
    chip, core = lax.div(gz, 2), lax.rem(gz, 2)
    rows_to = [gy] + [lax.rem(gy + dy, n_gy) for dy in range(1, n_gy)]
    chips_to = [chip] + [lax.rem(chip + dc, n_gz // 2) for dc in range(1, n_gz // 2)]
    me = gy * (n_gz // 2) + chip

    def peer(k):
        dy, dc = offsets[k]
        return rows_to[dy], chips_to[dc] * 2 + core

    has_low, has_high = gx > 0, gx < n_gx - 1
    x_low, x_high = jnp.maximum(gx - 1, 0), jnp.minimum(gx + 1, n_gx - 1)
    y_low, y_high = lax.rem(gy + n_gy - 1, n_gy), lax.rem(gy + 1, n_gy)
    z_low, z_high = lax.rem(gz + n_gz - 1, n_gz), lax.rem(gz + 1, n_gz)

    barrier = pltpu.get_barrier_semaphore()
    for k in range(chips - 1, 0, -1):
        pl.semaphore_signal(barrier, inc=1, device_id=(gx,) + peer(k), device_id_type=MESH)
    for z in (z_low, z_high):
        pl.semaphore_signal(barrier, inc=1, device_id=(gx, gy, z), device_id_type=MESH)
    for x, present in ((x_low, has_low), (x_high, has_high)):

        @pl.when(present)
        def _(x=x):
            pl.semaphore_signal(barrier, inc=1, device_id=(x, gy, gz), device_id_type=MESH)

    for i in (2, 1, 3, 0, 4, 5):
        loads[i].start()

    for side, present in ((0, has_low), (1, has_high)):

        @pl.when(jnp.logical_not(present))
        def _(side=side):
            for step in range(2):
                x_in[step, side] = jnp.zeros_like(x_in[step, side])

    sends_when = [has_low, has_high, None, None, None, None]
    comes_when = [has_high, has_low, None, None, None, None]

    def each(copies, conditions, act):
        for copy, condition in zip(copies, conditions):
            if condition is None:
                act(copy)
            else:
                pl.when(condition)(functools.partial(act, copy))

    def start_halos(copies):
        each(copies, sends_when, lambda copy: copy.start())

    def await_halos(copies):
        each(copies, comes_when, lambda copy: copy.wait_recv())


    lane = lax.broadcasted_iota(jnp.int32, (8, 128), 1)
    sub = lax.broadcasted_iota(jnp.int32, (8, 128), 0)

    def fill_halos(source, step):
        for f in range(5):
            y_out[step, 0, f] = source[f, :, 0, :]
            y_out[step, 1, f] = source[f, :, 7, :]
        packed = jnp.zeros((8, 128), F32)
        for f in range(5):
            for x in range(8):
                at = f * 8 + x
                packed = jnp.where(
                    lane // 2 == at, pltpu.roll(source[f, x], (1 + 2 * at) % 128, 1), packed
                )
        z_out[step] = packed

    def halo_copies(source, step):
        sides = [
            (source.at[:, 0], x_in.at[step, 1], (x_low, gy, gz)),
            (source.at[:, 7], x_in.at[step, 0], (x_high, gy, gz)),
            (y_out.at[step, 0], y_in.at[step, 1], (gx, y_low, gz)),
            (y_out.at[step, 1], y_in.at[step, 0], (gx, y_high, gz)),
            (z_out.at[step], z_in.at[step, 1], (gx, gy, z_low)),
            (z_out.at[step], z_in.at[step, 0], (gx, gy, z_high)),
        ]
        return [
            pltpu.make_async_remote_copy(
                src_ref=source_ref,
                dst_ref=target_ref,
                send_sem=halo_send.at[step, i],
                recv_sem=halo_recv.at[step, i],
                device_id=device,
                device_id_type=MESH,
            )
            for i, (source_ref, target_ref, device) in enumerate(sides)
        ]

    def inner(source):
        wind = [source[d].reshape(64, 128) for d in range(3)]
        for f in range(5):
            value = source[f].reshape(64, 128)
            high, low = halves(value)
            across = dot(planes[...], jnp.concatenate([high, low, high], 0))
            along = dot(jnp.concatenate([high, low], 1), line[...])
            total = value + wind[0] * across[:64] + wind[1] * across[64:]
            total = total + wind[2] * (along[:, :128] + along[:, 128:])
            part[f] = total.reshape(8, 8, 128)

    lift = LIFT * TIME_STEP
    x_prev = jnp.where(gx == 0, 0.0, lift)
    x_next = jnp.where(gx == n_gx - 1, 0.0, -lift)
    y_prev = jnp.where(sub == 0, jnp.where(gy == 0, 0.0, lift), 0.0)
    y_next = jnp.where(sub == 7, jnp.where(gy == n_gy - 1, 0.0, -lift), 0.0)
    z_side = jnp.where(lane == 0, lift, 0.0) + jnp.where(lane == 127, -lift, 0.0)

    def outer(source, target, step, which=range(5)):
        merged = jnp.where(
            lane % 2 == 0,
            pltpu.roll(z_in[step, 1], 127, 1),
            pltpu.roll(z_in[step, 0], 1, 1),
        )
        for x in range(8):
            wind = [source[d, x] for d in range(3)]
            y_wind = (wind[1] * y_prev, wind[1] * y_next)
            z_wind = wind[2] * z_side
            for f in which:
                at = f * 8 + x
                total = part[f, x]
                if x == 0:
                    total = total + wind[0] * (x_prev * x_in[step, 0, f])
                if x == 7:
                    total = total + wind[0] * (x_next * x_in[step, 1, f])
                total = total + y_wind[0] * y_in[step, 0, f, pl.ds(x, 1), :]
                total = total + y_wind[1] * y_in[step, 1, f, pl.ds(x, 1), :]
                total = total + z_wind * pltpu.roll(merged, (127 - 2 * at) % 128, 1)
                target[f, x] = total

    for load in loads[1:4]:
        load.wait()
    place_of = jnp.bitwise_xor(owner[...], core).astype(F32)
    square = jnp.broadcast_to(place_of, (blocks, blocks))
    diagonal = lax.broadcasted_iota(jnp.int32, (blocks, blocks), 0) == lax.broadcasted_iota(
        jnp.int32, (blocks, blocks), 1
    )
    owner_column = jnp.sum(jnp.where(diagonal, square, 0.0), axis=1, keepdims=True)
    owner_column = jnp.broadcast_to(owner_column, (blocks, 128))
    row = lax.broadcasted_iota(jnp.int32, (blocks, 128), 0)
    column = lax.broadcasted_iota(jnp.int32, (blocks, 128), 1)
    block_lane = lax.rem(column, blocks)
    owner_lane = jnp.sum(jnp.where(row == block_lane, owner_column, 0.0), axis=0, keepdims=True)
    same = owner_column == owner_lane
    earlier_lane = jnp.sum(
        jnp.where(same & (row < block_lane), 1.0, 0.0), axis=0, keepdims=True
    )
    earlier_column = jnp.sum(
        jnp.where(same & (column < row), 1.0, 0.0), axis=1, keepdims=True
    )
    slot_lane = owner_lane * 8.0 + earlier_lane * 4.0
    slot_column = owner_column[:, :1] * 8.0 + earlier_column * 4.0
    slots[...] = jnp.broadcast_to(slot_column, (blocks, 128))
    for b in range(blocks):
        payload[pl.ds(b, 3, stride=blocks), :] = tracer[:, b * 128 : (b + 1) * 128]
    payload[3 * blocks :, :] = host[...].astype(F32)
    width = 4 * blocks
    tall = lax.broadcasted_iota(jnp.int32, (group * 8, width), 0).astype(F32)
    part_lane = lax.broadcasted_iota(jnp.int32, (1, width), 1) // blocks
    target_row = slot_lane[:, :width] + part_lane.astype(F32)
    place = jnp.where(tall == target_row, 1.0, 0.0).astype(BF16)
    high, low = halves(payload[...])
    packed = dot(
        jnp.concatenate([place, place], 1), jnp.concatenate([high, low], 0)
    )
    outgoing[...] = packed

    loads[4].wait()
    loads[5].wait()
    high, low = halves(planes_f32[...])
    planes[...] = jnp.concatenate([high, high, low], 1)
    high, low = halves(line_f32[...])
    line[:128, :128] = high
    line[128:, :128] = high
    line[:128, 128:] = low
    line[128:, 128:] = jnp.zeros_like(low)

    loads[0].wait()
    fill_halos(state, 0)

    pl.semaphore_wait(barrier, chips + 1 + has_low.astype(jnp.int32) + has_high.astype(jnp.int32))

    def send_block(k):
        to_y, to_z = peer(k)
        pltpu.make_async_remote_copy(
            src_ref=outgoing.at[
                pl.ds(pl.multiple_of((to_y * (n_gz // 2) + lax.div(to_z, 2)) * 16, 16), 16)
            ],
            dst_ref=received.at[pl.ds(opposite[k] * 16, 16)],
            send_sem=route_send.at[0],
            recv_sem=route_recv.at[0, ring_of(k)],
            device_id=(gx, to_y, to_z),
            device_id_type=MESH,
        ).start()

    def ring_of(k):
        return [i for i, ring in enumerate(rings) if k in ring][0]

    far = [k for ring in rings[3:][::-1] for k in ring]
    near = [k for ring in rings[:3][::-1] for k in ring if k > 0]
    first = halo_copies(state, 0)
    start_halos(first)
    for k in far:
        send_block(k)
    for k in near:
        send_block(k)
    received[0:16, :] = outgoing[pl.ds(pl.multiple_of(me * 16, 16), 16), :]

    inner(state)
    await_halos(first)
    outer(state, half, 0, range(3))
    partner = pltpu.make_async_remote_copy(
        src_ref=half.at[pl.ds(0, 3)],
        dst_ref=sibling,
        send_sem=table_sem.at[0],
        recv_sem=table_sem.at[1],
        device_id=(gx, gy, chip * 2 + 1 - core),
        device_id_type=MESH,
    )
    partner.start()
    outer(state, half, 0, range(3, 5))
    fill_halos(half, 1)
    second = halo_copies(half, 1)
    start_halos(second)

    tables[0] = half[0:3].reshape(192, 128).astype(BF16)
    lower_half = jnp.where(lax.broadcasted_iota(jnp.int32, (16, 128), 0) >= 8, 1.0, 0.0)

    points = gll_nodes()
    scales = [
        float(1.0 / np.prod([points[n] - points[m] for m in range(8) if m != n])) for n in range(8)
    ]

    def lagrange(coordinate):
        steps = [coordinate - float(points[m]) for m in range(8)]
        before, after = [None, steps[0]], [None, steps[7]]
        for m in range(1, 7):
            before.append(before[-1] * steps[m])
            after.append(after[-1] * steps[7 - m])
        after = after[::-1]
        values = [after[0]] + [before[n] * after[n] for n in range(1, 7)] + [before[7]]
        return [value * scale for value, scale in zip(values, scales)]

    def weigh(p):
        for c in range(3):
            for n, value in enumerate(lagrange(received[pl.ds(p * 32 + c, 8, stride=4), :])):
                factors[pl.ds(pl.multiple_of(p * 192 + c * 64 + n * 8, 8), 8), :] = value
        for at in range(8):
            lanes = slice((at % 2) * 128, (at % 2 + 1) * 128)
            along = factors[pl.ds(p * 192 + 128 + at, 8, stride=8), :]
            pair = jnp.concatenate([along, along], 0).astype(BF16)
            even = (received[pl.ds(p * 32 + at * 4 + 3, 1), :] - lower_half).astype(BF16)
            for e in range(8):
                z_weights[p * 4 + at // 2, e * 16 : (e + 1) * 16, lanes] = jnp.where(
                    even == jnp.asarray(2 * e, BF16), pair, jnp.zeros_like(pair)
                )

    def interpolate(k, owner):
        s = 2 * k + owner
        values = dot(tables[owner], z_weights[s])
        for a in range(2):
            lanes = slice(a * 128, (a + 1) * 128)
            base = (k // 2) * 192 + (k % 2) * 4 + owner * 2 + a
            across = factors[pl.ds(base + 64, 8, stride=8), :]
            rows = []
            for c in range(3):
                total = None
                for i in range(8):
                    at = c * 64 + i * 8
                    term = factors[base + i * 8 : base + i * 8 + 1, :] * values[at : at + 8, lanes]
                    total = term if total is None else total + term
                rows.append(jnp.sum(total * across, axis=0, keepdims=True))
            velocity[k, owner, 4 * a : 4 * a + 4, :] = jnp.concatenate(rows + [jnp.zeros_like(rows[0])], 0)

    def await_ring(i):
        span = received.at[pl.ds(0, 16 * len(rings[i]))]
        pltpu.make_async_copy(span, span, route_recv.at[0, i]).wait()

    def weigh_pairs(first_pair, end_pair):
        def step(p, carry):
            weigh(p)
            return carry

        lax.fori_loop(first_pair, end_pair, step, 0)

    def weigh_ring(i):
        await_ring(i)
        if i == len(rings) - 1:
            weigh_pairs(0, 1)
        else:
            weigh_pairs(rings[i][0] // 2, (rings[i][-1] + 1) // 2)

    def apply(table, *which):
        for i in which:
            for k in rings[i]:
                interpolate(k, table)

    def answer(*which):
        ks = [k for i in which for k in rings[i]]
        for k in ks:
            if k == 0:
                returned[me] = velocity[0]
                continue
            pltpu.make_async_remote_copy(
                src_ref=velocity.at[k],
                dst_ref=returned.at[me],
                send_sem=route_send.at[1],
                recv_sem=route_recv.at[1, 0],
                device_id=(gx,) + peer(k),
                device_id_type=MESH,
            ).start()

    last = len(rings) - 1
    far_rings = tuple(range(last, max(last - 2, 1), -1))
    middle = tuple(range(min(far_rings) - 1, 1, -1))
    weigh_ring(1)
    apply(0, 1)
    for i in far_rings[::-1]:
        weigh_ring(i)
    apply(0, *far_rings)
    partner.wait_recv()
    tables[1] = sibling[...].reshape(192, 128).astype(BF16)
    apply(1, *far_rings)
    answer(*far_rings)
    for i in middle:
        weigh_ring(i)
        apply(0, i)
        apply(1, i)
        answer(i)
    apply(0, 0)
    apply(1, 1, 0)
    answer(1, 0)

    inner(half)
    await_halos(second)
    outer(half, final, 1)

    others = returned.at[pl.ds(0, chips - 1)]
    pltpu.make_async_copy(others, others, route_recv.at[1, 0]).wait()
    partner.wait_send()
    for copies in (first, second):
        each(copies, sends_when, lambda copy: copy.wait_send())
    others = outgoing.at[pl.ds(0, 16 * (chips - 1))]
    pltpu.make_async_copy(others, others, route_send.at[0]).wait()
    others = velocity.at[pl.ds(0, chips - 1)]
    pltpu.make_async_copy(others, others, route_send.at[1]).wait()


def finish(final, returned, tracer, slots, final_hbm, moved_hbm, own_velocity, moved, store_sem):
    store = pltpu.make_async_copy(final, final_hbm, store_sem.at[0])
    store.start()
    blocks, group = slots.shape[0], 2 * returned.shape[0]
    high, low = halves(returned[...].reshape(group * 8, 128))
    wide = lax.broadcasted_iota(jnp.int32, (blocks, group * 8), 1).astype(F32)
    unpack = jnp.concatenate(
        [jnp.where(wide == slots[:, :1] + float(c), 1.0, 0.0).astype(BF16) for c in range(3)], 0
    )
    own_velocity[...] = dot(unpack, high) + dot(unpack, low)
    for b in range(blocks):
        lanes = slice(b * 128, (b + 1) * 128)
        moved[:, lanes] = (
            tracer[:, lanes] + ADVANCE * own_velocity[pl.ds(b, 3, stride=blocks), :]
        )
    store_moved = pltpu.make_async_copy(moved, moved_hbm, store_sem.at[1])
    store_moved.start()
    store.wait()
    store_moved.wait()


def shards(sizes, fields, tracer_ref, host_element, block_owner):
    n_gx, n_gy, n_gz = sizes
    group, chips = n_gy * n_gz, n_gy * (n_gz // 2)
    blocks = block_owner.shape[0]
    planes, line = constants()
    arrays = (
        fields,
        tracer_ref,
        host_element.reshape(blocks, 128),
        block_owner.reshape(1, blocks),
        jnp.asarray(planes),
        jnp.asarray(line),
    )
    in_hbm = pl.BlockSpec(memory_space=pltpu.HBM)
    in_vmem = pl.BlockSpec(memory_space=pltpu.VMEM)
    results = pl.pallas_call(
        functools.partial(body, (n_gx, n_gy, n_gz, blocks)),
        out_shape=(
            jax.ShapeDtypeStruct(fields.shape, F32),
            jax.ShapeDtypeStruct((chips, 2, 8, 128), F32),
            jax.ShapeDtypeStruct(tracer_ref.shape, F32),
            jax.ShapeDtypeStruct((blocks, 128), F32),
        ),
        in_specs=[in_hbm] * len(arrays),
        out_specs=(in_vmem,) * 4,
        scratch_shapes=[
            pltpu.VMEM(fields.shape, F32),
            pltpu.VMEM(fields.shape, F32),
            pltpu.VMEM(fields.shape, F32),
            pltpu.VMEM((blocks, 128), jnp.int32),
            pltpu.VMEM((1, blocks), jnp.int32),
            pltpu.VMEM(planes.shape, F32),
            pltpu.VMEM(line.shape, F32),
            pltpu.VMEM((128, 192), BF16),
            pltpu.VMEM((256, 256), BF16),
            pltpu.VMEM((2, 2, 5, 8, 128), F32),
            pltpu.VMEM((2, 8, 128), F32),
            pltpu.VMEM((2, 2, 5, 8, 128), F32),
            pltpu.VMEM((2, 2, 5, 8, 128), F32),
            pltpu.VMEM((2, 2, 8, 128), F32),
            pltpu.VMEM((4 * blocks, 128), F32),
            pltpu.VMEM((group * 8, 128), F32),
            pltpu.VMEM((group * 8, 128), F32),
            pltpu.VMEM((group, 128, 256), BF16),
            pltpu.VMEM((chips // 2 * 192, 128), F32),
            pltpu.VMEM((chips, 2, 8, 128), F32),
            pltpu.VMEM((3, 8, 8, 128), F32),
            pltpu.VMEM((2, 192, 128), BF16),
            pltpu.SemaphoreType.DMA((len(arrays),)),
            pltpu.SemaphoreType.DMA((2, 6)),
            pltpu.SemaphoreType.DMA((2, 6)),
            pltpu.SemaphoreType.DMA((2,)),
            pltpu.SemaphoreType.DMA((2, 8)),
            pltpu.SemaphoreType.DMA((2,)),
        ],
        compiler_params=pltpu.CompilerParams(
            collective_id=0, has_side_effects=True, vmem_limit_bytes=40 * 1024 * 1024
        ),
    )(*[pltpu.with_memory_space_constraint(array, pltpu.HBM) for array in arrays])
    return pl.pallas_call(
        finish,
        out_shape=(
            jax.ShapeDtypeStruct(fields.shape, F32),
            jax.ShapeDtypeStruct(tracer_ref.shape, F32),
        ),
        in_specs=[in_vmem] * 4,
        out_specs=(in_hbm, in_hbm),
        scratch_shapes=[
            pltpu.VMEM((3 * blocks, 128), F32),
            pltpu.VMEM(tracer_ref.shape, F32),
            pltpu.SemaphoreType.DMA((2,)),
        ],
        compiler_params=pltpu.CompilerParams(vmem_limit_bytes=2 * 1024 * 1024),
    )(*results)


def solution(mesh):
    sizes = tuple(mesh.shape[axis] for axis in ("gx", "gy", "gz"))
    return jax.shard_map(
        functools.partial(shards, sizes),
        mesh=mesh,
        in_specs=(
            P(None, "gx", "gy", "gz"),
            P(None, ("gx", "gy", "gz")),
            P(("gx", "gy", "gz")),
            P(("gx", "gy", "gz"), None),
        ),
        out_specs=(P(None, "gx", "gy", "gz"), P(None, ("gx", "gy", "gz"))),
        check_vma=False,
    )
```

```python
import functools

import jax
import jax.numpy as jnp
import numpy as np
from jax import lax
from jax.experimental import pallas as pl
from jax.experimental.pallas import tpu as pltpu
from jax.sharding import PartitionSpec as P

TIME_STEP = 0.01
LIFT = 14.0
ADVANCE = 0.5
F32 = jnp.float32
BF16 = jnp.bfloat16
MESH = pl.DeviceIdType.MESH


def gll_nodes():
    return np.array(
        [
            -1.0,
            -0.8717401485096066,
            -0.5917001814331423,
            -0.2092992179024789,
            0.2092992179024789,
            0.5917001814331423,
            0.8717401485096066,
            1.0,
        ]
    )


def legendre_seven(value):
    lower = 1.0
    upper = value
    for order in range(1, 7):
        lower, upper = (upper, ((2 * order + 1) * value * upper - order * lower) / (order + 1))
    return upper


def derivative_matrix():
    points = gll_nodes()
    legendre_at = [legendre_seven(float(points[i])) for i in range(8)]
    matrix = np.zeros((8, 8))
    for i in range(8):
        for m in range(8):
            if i != m:
                matrix[i, m] = legendre_at[i] / (legendre_at[m] * (points[i] - points[m]))
    matrix[0, 0] = -14.0
    matrix[7, 7] = 14.0
    return matrix


def constants():
    element = -derivative_matrix()
    element[0, 0] -= LIFT
    element[7, 7] += LIFT
    element = element * TIME_STEP
    eye = np.eye(8)
    planes = np.concatenate([np.kron(element, eye), np.kron(eye, element)], 0)
    line = np.kron(np.eye(16), element)
    for e in range(1, 16):
        line[8 * e, 8 * e - 1] = LIFT * TIME_STEP
        line[8 * e - 1, 8 * e] = -LIFT * TIME_STEP
    line = line.T
    return planes.astype(np.float32), line.astype(np.float32)


def slab_offsets(rows, chips):
    def distance(offset):
        dy, dc = offset
        return min(dy, rows - dy) + min(dc, chips - dc)

    every = [(dy, dc) for dy in range(rows) for dc in range(chips)]
    farthest = max(distance(offset) for offset in every)
    offsets = sorted(
        every,
        key=lambda offset: (0.5 if distance(offset) == farthest else distance(offset),) + offset,
    )
    opposite = [offsets.index(((rows - dy) % rows, (chips - dc) % chips)) for dy, dc in offsets]
    rings = [
        [k for k, offset in enumerate(offsets) if distance(offset) == d]
        for d in range(farthest + 1)
    ]
    return offsets, opposite, rings


def halves(value):
    high = value.astype(BF16)
    low = (value - high.astype(F32)).astype(BF16)
    return high, low


def dot(a, b):
    return jnp.dot(a, b, preferred_element_type=F32)


def body(
    sizes,
    fields_hbm,
    tracer_hbm,
    host_hbm,
    owner_hbm,
    planes_hbm,
    line_hbm,
    final,
    returned,
    tracer,
    slots,
    state,
    half,
    part,
    host,
    owner,
    planes_f32,
    line_f32,
    planes,
    line,
    y_out,
    z_out,
    x_in,
    y_in,
    z_in,
    payload,
    outgoing,
    received,
    z_weights,
    factors,
    velocity,
    sibling,
    tables,
    load_sem,
    halo_send,
    halo_recv,
    route_send,
    route_recv,
    table_sem,
):
    n_gx, n_gy, n_gz, blocks = sizes
    group, chips = n_gy * n_gz, n_gy * (n_gz // 2)
    gx, gy, gz = lax.axis_index("gx"), lax.axis_index("gy"), lax.axis_index("gz")
    offsets, opposite, rings = slab_offsets(n_gy, n_gz // 2)

    loads = [
        pltpu.make_async_copy(source, target, load_sem.at[i])
        for i, (source, target) in enumerate(
            [
                (fields_hbm, state),
                (owner_hbm, owner),
                (tracer_hbm, tracer),
                (host_hbm, host),
                (planes_hbm, planes_f32),
                (line_hbm, line_f32),
            ]
        )
    ]
    chip, core = lax.div(gz, 2), lax.rem(gz, 2)
    rows_to = [gy] + [lax.rem(gy + dy, n_gy) for dy in range(1, n_gy)]
    chips_to = [chip] + [lax.rem(chip + dc, n_gz // 2) for dc in range(1, n_gz // 2)]
    me = gy * (n_gz // 2) + chip

    def peer(k):
        dy, dc = offsets[k]
        return rows_to[dy], chips_to[dc] * 2 + core

    has_low, has_high = gx > 0, gx < n_gx - 1
    x_low, x_high = jnp.maximum(gx - 1, 0), jnp.minimum(gx + 1, n_gx - 1)
    y_low, y_high = lax.rem(gy + n_gy - 1, n_gy), lax.rem(gy + 1, n_gy)
    z_low, z_high = lax.rem(gz + n_gz - 1, n_gz), lax.rem(gz + 1, n_gz)

    barrier = pltpu.get_barrier_semaphore()
    for k in range(chips - 1, 0, -1):
        pl.semaphore_signal(barrier, inc=1, device_id=(gx,) + peer(k), device_id_type=MESH)
    for z in (z_low, z_high):
        pl.semaphore_signal(barrier, inc=1, device_id=(gx, gy, z), device_id_type=MESH)
    for x, present in ((x_low, has_low), (x_high, has_high)):

        @pl.when(present)
        def _(x=x):
            pl.semaphore_signal(barrier, inc=1, device_id=(x, gy, gz), device_id_type=MESH)

    for i in (2, 1, 3, 0, 4, 5):
        loads[i].start()

    for side, present in ((0, has_low), (1, has_high)):

        @pl.when(jnp.logical_not(present))
        def _(side=side):
            for step in range(2):
                x_in[step, side] = jnp.zeros_like(x_in[step, side])

    sends_when = [has_low, has_high, None, None, None, None]
    comes_when = [has_high, has_low, None, None, None, None]

    def each(copies, conditions, act):
        for copy, condition in zip(copies, conditions):
            if condition is None:
                act(copy)
            else:
                pl.when(condition)(functools.partial(act, copy))

    def start_halos(copies):
        each(copies, sends_when, lambda copy: copy.start())

    def await_halos(copies):
        each(copies, comes_when, lambda copy: copy.wait_recv())


    lane = lax.broadcasted_iota(jnp.int32, (8, 128), 1)
    sub = lax.broadcasted_iota(jnp.int32, (8, 128), 0)

    def fill_halos(source, step):
        for f in range(5):
            y_out[step, 0, f] = source[f, :, 0, :]
            y_out[step, 1, f] = source[f, :, 7, :]
        packed = jnp.zeros((8, 128), F32)
        for f in range(5):
            for x in range(8):
                at = f * 8 + x
                packed = jnp.where(
                    lane // 2 == at, pltpu.roll(source[f, x], (1 + 2 * at) % 128, 1), packed
                )
        z_out[step] = packed

    def halo_copies(source, step):
        sides = [
            (source.at[:, 0], x_in.at[step, 1], (x_low, gy, gz)),
            (source.at[:, 7], x_in.at[step, 0], (x_high, gy, gz)),
            (y_out.at[step, 0], y_in.at[step, 1], (gx, y_low, gz)),
            (y_out.at[step, 1], y_in.at[step, 0], (gx, y_high, gz)),
            (z_out.at[step], z_in.at[step, 1], (gx, gy, z_low)),
            (z_out.at[step], z_in.at[step, 0], (gx, gy, z_high)),
        ]
        return [
            pltpu.make_async_remote_copy(
                src_ref=source_ref,
                dst_ref=target_ref,
                send_sem=halo_send.at[step, i],
                recv_sem=halo_recv.at[step, i],
                device_id=device,
                device_id_type=MESH,
            )
            for i, (source_ref, target_ref, device) in enumerate(sides)
        ]

    def inner(source):
        wind = [source[d].reshape(64, 128) for d in range(3)]
        for f in range(5):
            value = source[f].reshape(64, 128)
            high, low = halves(value)
            across = dot(planes[...], jnp.concatenate([high, low, high], 0))
            along = dot(jnp.concatenate([high, low], 1), line[...])
            total = value + wind[0] * across[:64] + wind[1] * across[64:]
            total = total + wind[2] * (along[:, :128] + along[:, 128:])
            part[f] = total.reshape(8, 8, 128)

    lift = LIFT * TIME_STEP
    x_prev = jnp.where(gx == 0, 0.0, lift)
    x_next = jnp.where(gx == n_gx - 1, 0.0, -lift)
    y_prev = jnp.where(sub == 0, jnp.where(gy == 0, 0.0, lift), 0.0)
    y_next = jnp.where(sub == 7, jnp.where(gy == n_gy - 1, 0.0, -lift), 0.0)
    z_side = jnp.where(lane == 0, lift, 0.0) + jnp.where(lane == 127, -lift, 0.0)

    def outer(source, target, step, which=range(5)):
        merged = jnp.where(
            lane % 2 == 0,
            pltpu.roll(z_in[step, 1], 127, 1),
            pltpu.roll(z_in[step, 0], 1, 1),
        )
        for x in range(8):
            wind = [source[d, x] for d in range(3)]
            y_wind = (wind[1] * y_prev, wind[1] * y_next)
            z_wind = wind[2] * z_side
            for f in which:
                at = f * 8 + x
                total = part[f, x]
                if x == 0:
                    total = total + wind[0] * (x_prev * x_in[step, 0, f])
                if x == 7:
                    total = total + wind[0] * (x_next * x_in[step, 1, f])
                total = total + y_wind[0] * y_in[step, 0, f, pl.ds(x, 1), :]
                total = total + y_wind[1] * y_in[step, 1, f, pl.ds(x, 1), :]
                total = total + z_wind * pltpu.roll(merged, (127 - 2 * at) % 128, 1)
                target[f, x] = total

    for load in loads[1:4]:
        load.wait()
    place_of = jnp.bitwise_xor(owner[...], core).astype(F32)
    square = jnp.broadcast_to(place_of, (blocks, blocks))
    diagonal = lax.broadcasted_iota(jnp.int32, (blocks, blocks), 0) == lax.broadcasted_iota(
        jnp.int32, (blocks, blocks), 1
    )
    owner_column = jnp.sum(jnp.where(diagonal, square, 0.0), axis=1, keepdims=True)
    owner_column = jnp.broadcast_to(owner_column, (blocks, 128))
    row = lax.broadcasted_iota(jnp.int32, (blocks, 128), 0)
    column = lax.broadcasted_iota(jnp.int32, (blocks, 128), 1)
    block_lane = lax.rem(column, blocks)
    owner_lane = jnp.sum(jnp.where(row == block_lane, owner_column, 0.0), axis=0, keepdims=True)
    same = owner_column == owner_lane
    earlier_lane = jnp.sum(
        jnp.where(same & (row < block_lane), 1.0, 0.0), axis=0, keepdims=True
    )
    earlier_column = jnp.sum(
        jnp.where(same & (column < row), 1.0, 0.0), axis=1, keepdims=True
    )
    slot_lane = owner_lane * 8.0 + earlier_lane * 4.0
    slot_column = owner_column[:, :1] * 8.0 + earlier_column * 4.0
    slots[...] = jnp.broadcast_to(slot_column, (blocks, 128))
    for b in range(blocks):
        payload[pl.ds(b, 3, stride=blocks), :] = tracer[:, b * 128 : (b + 1) * 128]
    payload[3 * blocks : 4 * blocks, :] = host[...].astype(F32)
    width = 4 * blocks
    tall = lax.broadcasted_iota(jnp.int32, (group * 8, width), 0).astype(F32)
    part_lane = lax.broadcasted_iota(jnp.int32, (1, width), 1) // blocks
    target_row = slot_lane[:, :width] + part_lane.astype(F32)
    place = jnp.where(tall == target_row, 1.0, 0.0).astype(BF16)
    high, low = halves(payload[0 : 4 * blocks, :])
    packed = dot(
        jnp.concatenate([place, place], 1), jnp.concatenate([high, low], 0)
    )
    outgoing[...] = packed

    loads[4].wait()
    loads[5].wait()
    high, low = halves(planes_f32[...])
    planes[...] = jnp.concatenate([high, high, low], 1)
    high, low = halves(line_f32[...])
    line[:128, :128] = high
    line[128:, :128] = high
    line[:128, 128:] = low
    line[128:, 128:] = jnp.zeros_like(low)

    loads[0].wait()
    fill_halos(state, 0)

    pl.semaphore_wait(barrier, chips + 1 + has_low.astype(jnp.int32) + has_high.astype(jnp.int32))

    def send_block(k):
        to_y, to_z = peer(k)
        pltpu.make_async_remote_copy(
            src_ref=outgoing.at[
                pl.ds(pl.multiple_of((to_y * (n_gz // 2) + lax.div(to_z, 2)) * 16, 16), 16)
            ],
            dst_ref=received.at[pl.ds(opposite[k] * 16, 16)],
            send_sem=route_send.at[0],
            recv_sem=route_recv.at[0, ring_of(k)],
            device_id=(gx, to_y, to_z),
            device_id_type=MESH,
        ).start()

    def ring_of(k):
        return [i for i, ring in enumerate(rings) if k in ring][0]

    far = [k for ring in rings[3:][::-1] for k in ring]
    near = [k for ring in rings[:3][::-1] for k in ring if k > 0]
    first = halo_copies(state, 0)
    start_halos(first)
    for k in far:
        send_block(k)
    for k in near:
        send_block(k)
    received[0:16, :] = outgoing[pl.ds(pl.multiple_of(me * 16, 16), 16), :]

    inner(state)
    await_halos(first)
    outer(state, half, 0, range(3))
    partner = pltpu.make_async_remote_copy(
        src_ref=half.at[pl.ds(0, 3)],
        dst_ref=sibling,
        send_sem=table_sem.at[0],
        recv_sem=table_sem.at[1],
        device_id=(gx, gy, chip * 2 + 1 - core),
        device_id_type=MESH,
    )
    partner.start()
    outer(state, half, 0, range(3, 5))
    fill_halos(half, 1)
    second = halo_copies(half, 1)
    start_halos(second)

    tables[0] = half[0:3].reshape(192, 128).astype(BF16)
    lower_half = jnp.where(lax.broadcasted_iota(jnp.int32, (16, 128), 0) >= 8, 1.0, 0.0)

    points = gll_nodes()
    scales = [
        float(1.0 / np.prod([points[n] - points[m] for m in range(8) if m != n])) for n in range(8)
    ]

    def lagrange(coordinate):
        steps = [coordinate - float(points[m]) for m in range(8)]
        before, after = [None, steps[0]], [None, steps[7]]
        for m in range(1, 7):
            before.append(before[-1] * steps[m])
            after.append(after[-1] * steps[7 - m])
        after = after[::-1]
        values = [after[0]] + [before[n] * after[n] for n in range(1, 7)] + [before[7]]
        return [value * scale for value, scale in zip(values, scales)]

    def weigh(p):
        for c in range(3):
            for n, value in enumerate(lagrange(received[pl.ds(p * 32 + c, 8, stride=4), :])):
                factors[pl.ds(pl.multiple_of(p * 192 + c * 64 + n * 8, 8), 8), :] = value
        for at in range(8):
            lanes = slice((at % 2) * 128, (at % 2 + 1) * 128)
            along = factors[pl.ds(p * 192 + 128 + at, 8, stride=8), :]
            pair = jnp.concatenate([along, along], 0).astype(BF16)
            even = (received[pl.ds(p * 32 + at * 4 + 3, 1), :] - lower_half).astype(BF16)
            for e in range(8):
                z_weights[p * 4 + at // 2, e * 16 : (e + 1) * 16, lanes] = jnp.where(
                    even == jnp.asarray(2 * e, BF16), pair, jnp.zeros_like(pair)
                )

    def interpolate(k, owner):
        s = 2 * k + owner
        values = dot(tables[owner], z_weights[s])
        for a in range(2):
            lanes = slice(a * 128, (a + 1) * 128)
            base = (k // 2) * 192 + (k % 2) * 4 + owner * 2 + a
            across = factors[pl.ds(base + 64, 8, stride=8), :]
            rows = []
            for c in range(3):
                total = None
                for i in range(8):
                    at = c * 64 + i * 8
                    term = factors[base + i * 8 : base + i * 8 + 1, :] * values[at : at + 8, lanes]
                    total = term if total is None else total + term
                rows.append(jnp.sum(total * across, axis=0, keepdims=True))
            velocity[k, owner, 4 * a : 4 * a + 4, :] = jnp.concatenate(rows + [jnp.zeros_like(rows[0])], 0)

    def await_ring(i):
        span = received.at[pl.ds(0, 16 * len(rings[i]))]
        pltpu.make_async_copy(span, span, route_recv.at[0, i]).wait()

    def weigh_pairs(first_pair, end_pair):
        def step(p, carry):
            weigh(p)
            return carry

        lax.fori_loop(first_pair, end_pair, step, 0)

    def weigh_ring(i):
        await_ring(i)
        if i == len(rings) - 1:
            weigh_pairs(0, 1)
        else:
            weigh_pairs(rings[i][0] // 2, (rings[i][-1] + 1) // 2)

    def apply(table, *which):
        for i in which:
            for k in rings[i]:
                interpolate(k, table)

    def answer(*which):
        ks = [k for i in which for k in rings[i]]
        for k in ks:
            if k == 0:
                returned[me] = velocity[0]
                continue
            pltpu.make_async_remote_copy(
                src_ref=velocity.at[k],
                dst_ref=returned.at[me],
                send_sem=route_send.at[1],
                recv_sem=route_recv.at[1, 0],
                device_id=(gx,) + peer(k),
                device_id_type=MESH,
            ).start()

    last = len(rings) - 1
    far_rings = tuple(range(last, max(last - 2, 1), -1))
    middle = tuple(range(min(far_rings) - 1, 1, -1))
    weigh_ring(1)
    apply(0, 1)
    for i in far_rings[::-1]:
        weigh_ring(i)
    apply(0, *far_rings)
    partner.wait_recv()
    tables[1] = sibling[...].reshape(192, 128).astype(BF16)
    apply(1, *far_rings)
    answer(*far_rings)
    for i in middle:
        weigh_ring(i)
        apply(0, i)
        apply(1, i)
        answer(i)
    apply(0, 0)
    apply(1, 1, 0)
    answer(1, 0)

    inner(half)
    await_halos(second)
    outer(half, final, 1)

    others = returned.at[pl.ds(0, chips - 1)]
    pltpu.make_async_copy(others, others, route_recv.at[1, 0]).wait()
    partner.wait_send()
    for copies in (first, second):
        each(copies, sends_when, lambda copy: copy.wait_send())
    others = outgoing.at[pl.ds(0, 16 * (chips - 1))]
    pltpu.make_async_copy(others, others, route_send.at[0]).wait()
    others = velocity.at[pl.ds(0, chips - 1)]
    pltpu.make_async_copy(others, others, route_send.at[1]).wait()


def finish(final, returned, tracer, slots, final_hbm, moved_hbm, own_velocity, moved, store_sem):
    store = pltpu.make_async_copy(final, final_hbm, store_sem.at[0])
    store.start()
    blocks, group = slots.shape[0], 2 * returned.shape[0]
    high, low = halves(returned[...].reshape(group * 8, 128))
    wide = lax.broadcasted_iota(jnp.int32, (blocks, group * 8), 1).astype(F32)
    unpack = jnp.concatenate(
        [jnp.where(wide == slots[:, :1] + float(c), 1.0, 0.0).astype(BF16) for c in range(3)], 0
    )
    own_velocity[0 : 3 * blocks, :] = dot(unpack, high) + dot(unpack, low)
    for b in range(blocks):
        lanes = slice(b * 128, (b + 1) * 128)
        moved[:, lanes] = (
            tracer[:, lanes] + ADVANCE * own_velocity[pl.ds(b, 3, stride=blocks), :]
        )
    store_moved = pltpu.make_async_copy(moved, moved_hbm, store_sem.at[1])
    store_moved.start()
    store.wait()
    store_moved.wait()


def shards(sizes, fields, tracer_ref, host_element, block_owner):
    n_gx, n_gy, n_gz = sizes
    group, chips = n_gy * n_gz, n_gy * (n_gz // 2)
    blocks = block_owner.shape[0]
    planes, line = constants()
    arrays = (
        fields,
        tracer_ref,
        host_element.reshape(blocks, 128),
        block_owner.reshape(1, blocks),
        jnp.asarray(planes),
        jnp.asarray(line),
    )
    in_hbm = pl.BlockSpec(memory_space=pltpu.HBM)
    in_vmem = pl.BlockSpec(memory_space=pltpu.VMEM)
    results = pl.pallas_call(
        functools.partial(body, (n_gx, n_gy, n_gz, blocks)),
        out_shape=(
            jax.ShapeDtypeStruct(fields.shape, F32),
            jax.ShapeDtypeStruct((chips, 2, 8, 128), F32),
            jax.ShapeDtypeStruct(tracer_ref.shape, F32),
            jax.ShapeDtypeStruct((blocks, 128), F32),
        ),
        in_specs=[in_hbm] * len(arrays),
        out_specs=(in_vmem,) * 4,
        scratch_shapes=[
            pltpu.VMEM(fields.shape, F32),
            pltpu.VMEM(fields.shape, F32),
            pltpu.VMEM(fields.shape, F32),
            pltpu.VMEM((blocks, 128), jnp.int32),
            pltpu.VMEM((1, blocks), jnp.int32),
            pltpu.VMEM(planes.shape, F32),
            pltpu.VMEM(line.shape, F32),
            pltpu.VMEM((128, 192), BF16),
            pltpu.VMEM((256, 256), BF16),
            pltpu.VMEM((2, 2, 5, 8, 128), F32),
            pltpu.VMEM((2, 8, 128), F32),
            pltpu.VMEM((2, 2, 5, 8, 128), F32),
            pltpu.VMEM((2, 2, 5, 8, 128), F32),
            pltpu.VMEM((2, 2, 8, 128), F32),
            pltpu.VMEM((9 * blocks, 128), F32),
            pltpu.VMEM((group * 8, 128), F32),
            pltpu.VMEM((group * 8 + 8, 128), F32),
            pltpu.VMEM((group, 128, 256), BF16),
            pltpu.VMEM((chips // 2 * 192 + 8, 128), F32),
            pltpu.VMEM((chips, 2, 8, 128), F32),
            pltpu.VMEM((3, 8, 8, 128), F32),
            pltpu.VMEM((2, 192, 128), BF16),
            pltpu.SemaphoreType.DMA((len(arrays),)),
            pltpu.SemaphoreType.DMA((2, 6)),
            pltpu.SemaphoreType.DMA((2, 6)),
            pltpu.SemaphoreType.DMA((2,)),
            pltpu.SemaphoreType.DMA((2, 8)),
            pltpu.SemaphoreType.DMA((2,)),
        ],
        compiler_params=pltpu.CompilerParams(
            collective_id=0, has_side_effects=True, vmem_limit_bytes=40 * 1024 * 1024
        ),
    )(*[pltpu.with_memory_space_constraint(array, pltpu.HBM) for array in arrays])
    return pl.pallas_call(
        finish,
        out_shape=(
            jax.ShapeDtypeStruct(fields.shape, F32),
            jax.ShapeDtypeStruct(tracer_ref.shape, F32),
        ),
        in_specs=[in_vmem] * 4,
        out_specs=(in_hbm, in_hbm),
        scratch_shapes=[
            pltpu.VMEM((9 * blocks, 128), F32),
            pltpu.VMEM(tracer_ref.shape, F32),
            pltpu.SemaphoreType.DMA((2,)),
        ],
        compiler_params=pltpu.CompilerParams(vmem_limit_bytes=2 * 1024 * 1024),
    )(*results)


def solution(mesh):
    sizes = tuple(mesh.shape[axis] for axis in ("gx", "gy", "gz"))
    return jax.shard_map(
        functools.partial(shards, sizes),
        mesh=mesh,
        in_specs=(
            P(None, "gx", "gy", "gz"),
            P(None, ("gx", "gy", "gz")),
            P(("gx", "gy", "gz")),
            P(("gx", "gy", "gz"), None),
        ),
        out_specs=(P(None, "gx", "gy", "gz"), P(None, ("gx", "gy", "gz"))),
        check_vma=False,
    )
```
